512 devices in a mesh: dp: 2 (over core), ctx: 32 (over x_hi, z), ch: 8 (over x_lo, y).
Axes of the slice: x: 4 (x_hi: 2, x_lo: 2; x = x_hi * 2 + x_lo), y: 4, z: 16, core: 2. Of those that a mesh axis runs over, the one named last changes fastest.
Arguments:
- query_proj: bfloat16 [8192, 8192], P(('dp', 'ctx'), 'ch'), may hold values from -6 to 6
- key_proj: bfloat16 [8192, 8192], P(('dp', 'ctx'), 'ch'), may hold values from -6 to 6
- value_proj: bfloat16 [8192, 8192], P(('dp', 'ctx'), 'ch'), may hold values from -6 to 6
- cotangent: bfloat16 [8192, 8192], P(('dp', 'ctx'), 'ch'), may hold values from -6 to 6
- filter_taps: bfloat16 [256, 8192], P(None, ('ch', 'ctx')), may hold values from -0.375 to 0.375
- span_slot: int32 [2, 32], P('dp'), may hold values from 0 to 31, each once within a row
- doc_lengths: int32 [2, 24], P('dp'), may hold values from 1 to 2, 32 in all within a row
Outputs:
- grad_query: bfloat16 [8192, 8192], P(('dp', 'ctx'), 'ch')
- grad_key: bfloat16 [8192, 8192], P(('dp', 'ctx'), 'ch')
- grad_value: bfloat16 [8192, 8192], P(('dp', 'ctx'), 'ch')
- grad_filter: bfloat16 [256, 8192], P(None, ('ch', 'ctx'))
The draws below stay inside these ranges and needn't reach their ends.
Inputs may be any that keep to these rules, and one draw needn't show every extreme that they name: Each row span_slot[w] is a permutation of the spans of window w. Each row doc_lengths[w] sums to 32 and holds 2 at least once.
All inputs are finite; a program needn't handle non-finite values.
Results may differ from the reference program's by a relative error of at most 0.012.
Values may be sent and summed in bfloat16 or wider, within the bound.
No kernel may reach another device: no remote copies, remote signals or barrier semaphores. Data moves between devices by JAX's collectives and lax.ppermute only.
A program may use at most 64 MiB of HBM per device.

```python
import math
import jax
import jax.numpy as jnp
import numpy as np
from jax import lax

D = 8192
SPAN = 128
TOK_DEV = 128
DOCMAX = 2
FILT = 256
NCHUNK = 32
NDOC = 24
TOKENS = 8192
N_DP = 2
N_CTX = 32


def shard_levels(key, dims, cuts, least, high):
    def one(axis_at, parts):
        heights = jax.random.uniform(jax.random.fold_in(jax.random.fold_in(key, 6), axis_at), (parts,), jnp.float32, least / len(cuts), high / len(cuts))
        return jnp.repeat(jnp.exp(heights), dims[axis_at] // parts).reshape((-1,) + (1,) * (len(dims) - axis_at - 1))

    loudness = one(*cuts[0])
    for cut in cuts[1:]:
        loudness = loudness * one(*cut)
    return loudness


def split_up(number_of, total, most, skew):
    loads = [(1 << 20) // math.isqrt(standing ** skew) + 1 for standing in range(2, number_of + 1)]
    spare, given = total - most - (number_of - 1), [1] * (number_of - 1)
    while spare > 0:
        candidates = [i for i in range(number_of - 1) if given[i] < most]
        mass, budget = sum([loads[i] for i in candidates]), spare
        for i in candidates:
            addition = min(most - given[i], max(1, budget * loads[i] // mass), spare)
            given[i] = given[i] + addition
            spare = spare - addition
    return np.array([most] + given)


def uneven_parts(own_key, count, total, limit, skew):
    if count == 2:
        one = jax.random.randint(own_key, (), max(1, total - limit), min(limit, total - 1) + 1)
        return jnp.stack([one, total - one])
    sizes = jnp.asarray(split_up(count, total, limit, skew), jnp.int32)
    couples = (count - 1) // 2
    donor, receiver = sizes[1:1 + 2 * couples:2], sizes[2:2 + 2 * couples:2]
    margin = jnp.minimum(donor - 1, limit - receiver)
    moved = jax.random.randint(jax.random.fold_in(own_key, 1), (couples,), 0, 1 << 20) % (margin + 1)
    sizes = sizes.at[1:1 + 2 * couples:2].set(donor - moved).at[2:2 + 2 * couples:2].set(receiver + moved)
    return sizes[jax.random.permutation(jax.random.fold_in(own_key, 2), count)]


def normal_values(stream_key, extent, scale, limit, split=(), held_as=jnp.bfloat16):
    values = scale * jax.random.normal(stream_key, extent, jnp.float32)
    if split:
        values = values * shard_levels(stream_key, extent, split, -0.22, 0.18)
    return jnp.clip(values, -limit, limit).astype(held_as)


def setup_inputs(seed: int = 0) -> dict:
    seeds = jax.random.split(jax.random.key(seed), 8)
    query_proj = normal_values(seeds[0], (TOKENS, D), 1.0, 6.0, ((0, 64), (1, 8)))
    key_proj = normal_values(seeds[1], (TOKENS, D), 1.0, 6.0, ((0, 64), (1, 8)))
    value_proj = normal_values(seeds[2], (TOKENS, D), 1.0, 6.0, ((0, 64), (1, 8)))
    cotangent = normal_values(seeds[3], (TOKENS, D), 1.0, 6.0, ((0, 64), (1, 8)))
    filter_taps = normal_values(seeds[4], (FILT, D), FILT ** -0.5, 0.375, ((1, 256),))
    span_slot = jax.vmap(lambda own: jax.random.permutation(own, NCHUNK))(jax.random.split(seeds[5], N_DP)).reshape((N_DP, NCHUNK)).astype(jnp.int32)
    doc_lengths = jax.vmap(lambda own: uneven_parts(own, NDOC, NCHUNK, DOCMAX, 2))(jax.random.split(seeds[6], N_DP)).reshape((N_DP, NDOC)).astype(jnp.int32)
    return {"query_proj": query_proj, "key_proj": key_proj, "value_proj": value_proj, "cotangent": cotangent, "filter_taps": filter_taps, "span_slot": span_slot, "doc_lengths": doc_lengths}


def rounded(array):
    return lax.optimization_barrier(array.astype(jnp.bfloat16)).astype(jnp.float32)

def doc_starts(lengths_row, spans):
    starts = jnp.cumsum(lengths_row) - lengths_row
    span_ids = jnp.arange(spans, dtype=jnp.int32)
    inside = starts[None, :] <= span_ids[:, None]
    return lax.optimization_barrier(jnp.max(jnp.where(inside, starts[None, :], 0), axis=1)).astype(jnp.int32)

def block_conv(series, kernel, starts):
    spans, block_len, width = series.shape
    length = kernel.shape[0]
    blocks = (length + block_len - 2) // block_len + 1
    extended = jnp.concatenate([jnp.zeros((block_len, width), jnp.float32), kernel, jnp.zeros(((blocks + 1) * block_len - length, width), jnp.float32)], axis=0)
    offsets = np.arange(block_len)[:, None] - np.arange(block_len)[None, :] + block_len
    span_ids = jnp.arange(spans, dtype=jnp.int32)
    summed = jnp.zeros(series.shape, jnp.float32)
    for lag_block in range(blocks):
        toeplitz = extended[offsets + lag_block * block_len]
        shifted = jnp.concatenate([jnp.zeros((lag_block, block_len, width), jnp.float32), series[:spans - lag_block]], axis=0)
        allowed = (span_ids - lag_block >= starts).astype(jnp.float32)
        product = jnp.einsum('tsc,jsc->jtc', toeplitz, shifted, precision=lax.Precision.HIGHEST)
        summed = summed + allowed[:, None, None] * product
    return summed

def reference(query_proj, key_proj, value_proj, cotangent, filter_taps, span_slot, doc_lengths):
    window = TOK_DEV * N_CTX
    spans = window // SPAN
    group = math.gcd(D, 256)
    groups = D // group
    inverse = jnp.argsort(span_slot, axis=1).astype(jnp.int32)
    starts = jax.vmap(lambda row: doc_starts(row, spans))(doc_lengths)
    scale = TOKENS ** (-0.5)

    def to_blocks(array):
        shaped = array.reshape(N_DP, spans, SPAN, groups, group)
        ordered = jnp.take_along_axis(shaped, inverse[:, :, None, None, None], axis=1)
        return jnp.transpose(ordered, (3, 0, 1, 2, 4))

    def from_blocks(array):
        shaped = jnp.transpose(array, (1, 2, 3, 0, 4))
        placed = jnp.take_along_axis(shaped, span_slot[:, :, None, None, None], axis=1)
        return placed.reshape(TOKENS, D)
    taps = jnp.transpose(filter_taps.reshape(FILT, groups, group), (1, 0, 2))

    def convolve(series, kernel):
        return jax.vmap(block_conv, in_axes=(0, None, 0))(series, kernel, starts)

    def one_group(operands):
        query_blk, key_blk, value_blk, cot_blk, tap_blk = operands
        mixer = rounded(key_blk.astype(jnp.float32) * value_blk.astype(jnp.float32))
        mixed, pullback = jax.vjp(convolve, mixer, tap_blk.astype(jnp.float32))
        grad_q = (cot_blk.astype(jnp.float32) * rounded(mixed)).astype(jnp.bfloat16)
        grad_mix = rounded(cot_blk.astype(jnp.float32) * query_blk.astype(jnp.float32))
        grad_series, grad_kernel = pullback(grad_mix)
        grad_series = rounded(grad_series)
        grad_k = (grad_series * value_blk.astype(jnp.float32)).astype(jnp.bfloat16)
        grad_v = (grad_series * key_blk.astype(jnp.float32)).astype(jnp.bfloat16)
        return (grad_q, grad_k, grad_v, (grad_kernel * scale).astype(jnp.bfloat16))
    grad_q, grad_k, grad_v, grad_f = lax.map(one_group, (to_blocks(query_proj), to_blocks(key_proj), to_blocks(value_proj), to_blocks(cotangent), taps))
    grad_filter = jnp.transpose(grad_f, (1, 0, 2)).reshape(FILT, D)
    return (from_blocks(grad_q), from_blocks(grad_k), from_blocks(grad_v), grad_filter)
```

```python
import functools

import jax
import jax.numpy as jnp
import numpy as np
from jax import lax
from jax.experimental import pallas as pl
from jax.experimental.pallas import tpu as pltpu
from jax.sharding import PartitionSpec as P

SPAN = 128
PTS = 2 * SPAN
HALF = SPAN // 2
F32, BF16 = jnp.float32, jnp.bfloat16


def split_bf16(matrix):
    high = matrix.astype(BF16)
    low = (matrix - high.astype(np.float64)).astype(BF16)
    return high, low


def transforms():
    freq = np.arange(SPAN)[:, None]
    point = np.arange(PTS)[None, :]
    angle = 2 * np.pi * ((freq * point) % PTS) / PTS
    real, imag = np.cos(angle), -np.sin(angle)
    imag[0] = np.where(np.arange(PTS) % 2 == 0, 1.0, -1.0)
    forward = np.concatenate([real, imag], 0)
    weight = np.full((PTS, 1), 2.0 / PTS)
    weight[0], weight[SPAN] = 1.0 / PTS, 1.0 / PTS
    inverse = (forward * weight).T
    return forward, inverse


def dot(a, b, dims=((1,), (0,))):
    return lax.dot_general(a, b, (dims, ((), ())), preferred_element_type=F32)


def halves(x):
    high = x.astype(BF16)
    return high, (x - high.astype(F32)).astype(BF16)


def spectrum_left(high, low, x):
    return dot(high, x) + dot(low, x)


def spectrum_right(x, high, low):
    return dot(x, high) + dot(x, low)


def invert_left(high, low, spec):
    s_high, s_low = halves(spec)
    return dot(high, s_high) + (dot(high, s_low) + dot(low, s_high))


def invert_right(spec, high, low):
    s_high, s_low = halves(spec)
    return dot(s_high, high) + (dot(s_low, high) + dot(s_high, low))


def multiply(ar, ai, br, bi, zero, sign):
    b_im = sign * jnp.where(zero, 0.0, bi)
    b_second = jnp.where(zero, bi, br)
    return ar * br - ai * b_im, ai * b_second + ar * b_im


def pack_halves(lo, hi):
    axis = lo.ndim - 1
    left = lax.broadcasted_iota(jnp.int32, lo.shape, axis) < HALF
    first = jnp.where(left, lo, pltpu.roll(hi, HALF, axis))
    second = jnp.where(left, pltpu.roll(lo, HALF, axis), hi)
    return first, second


def own_kind(slot_ref, len_ref):
    span = slot_ref[0, lax.axis_index("ctx")]

    def step(d, carry):
        pos, kind = carry
        length = len_ref[0, d]
        two = length == 2
        kind = jnp.where(two & (span == pos), 1, kind)
        kind = jnp.where(two & (span == pos + 1), 2, kind)
        return pos + length, kind

    zero = jnp.int32(0)
    return lax.fori_loop(0, len_ref.shape[1], step, (zero, zero))[1]


def send_kernel(slot_ref, len_ref, taps_ref, q_ref, k_ref, v_ref, c_ref, out_ref):
    kind = own_kind(slot_ref, len_ref)
    count = out_ref.shape[0]

    def put(a_ref, b_ref):
        product = a_ref[...].astype(F32) * b_ref[...].astype(F32)
        out_ref[:, 0:32, :] = jnp.transpose(product).astype(BF16).reshape(count, 32, SPAN)

    @pl.when(kind == 1)
    def _():
        put(k_ref, v_ref)

    @pl.when(kind != 1)
    def _():
        put(c_ref, q_ref)

    taps = jnp.transpose(taps_ref[0:SPAN, :].astype(F32))
    first, second = pack_halves(taps[0:16], taps[16:32])
    mine = jnp.where(lax.axis_index("dp") == 0, first, second).astype(BF16)
    out_ref[:, 32:48, :] = jnp.broadcast_to(mine[None], (count, 16, SPAN))


def partial_kernel(
    slot_ref, len_ref, q_ref, k_ref, v_ref, c_ref, fwd_hi, fwd_lo, inv_hi, inv_lo,
    keep_ref, send_ref, table_ref, inverse_ref,
):
    @pl.when(pl.program_id(0) == 0)
    def _():
        slots = slot_ref.shape[1]

        def fill(r, carry):
            inverse_ref[slot_ref[0, r]] = r
            return carry

        lax.fori_loop(0, slots, fill, 0)

        def step(d, pos):
            length = len_ref[0, d]
            two = length == 2
            a = inverse_ref[pos]
            b = inverse_ref[jnp.minimum(pos + 1, slots - 1)]
            table_ref[0, a] = jnp.where(two, 1, 0)
            table_ref[1, a] = jnp.where(two, b, a)

            @pl.when(two)
            def _():
                table_ref[0, b] = -1
                table_ref[1, b] = a

            return pos + length

        lax.fori_loop(0, len_ref.shape[1], step, jnp.int32(0))

    x = (k_ref[...].astype(F32) * v_ref[...].astype(F32)).astype(BF16)
    g = (c_ref[...].astype(F32) * q_ref[...].astype(F32)).astype(BF16)
    xs = spectrum_left(fwd_hi[...], fwd_lo[...], x)
    gs = spectrum_left(fwd_hi[...], fwd_lo[...], g)
    shape = (SPAN, x.shape[1])
    zero = lax.broadcasted_iota(jnp.int32, shape, 0) == 0
    pr, pi = multiply(gs[:SPAN], gs[SPAN:], xs[:SPAN], xs[SPAN:], zero, -1.0)
    taps = invert_left(inv_hi[...], inv_lo[...], jnp.concatenate([pr, pi], 0))
    count = keep_ref.shape[0]
    rows = jnp.transpose(taps).reshape(count, 32, SPAN)
    first, second = pack_halves(rows[:, 0:16], rows[:, 16:32])
    is_first = lax.axis_index("dp") == 0
    keep_ref[...] = jnp.where(is_first, first, second)
    send_ref[...] = jnp.where(is_first, second, first).astype(BF16)


def pair_kernel(
    table_ref, got_ref, taps_ref, keep_ref, other_ref, fwd_hi, fwd_lo, inv_hi, inv_lo,
    tap_hi, tap_lo, out_ref, spec_ref,
):
    slots = got_ref.shape[0]
    taps = jnp.transpose(taps_ref[...].astype(F32)).astype(BF16)
    hs = spectrum_right(taps, tap_hi[...], tap_lo[...])
    hr, hi = hs[:, :SPAN], hs[:, SPAN:]
    zero = lax.broadcasted_iota(jnp.int32, hr.shape, 1) == 0
    h_im = jnp.where(zero, 0.0, hi)
    h_second = jnp.where(zero, hi, hr)
    series = got_ref[:, 0:32, :].reshape(slots * 32, SPAN)
    spec = spectrum_right(series, fwd_hi[...], fwd_lo[...])
    spec = spec.reshape(slots, 32, PTS)
    for p in range(slots):
        sign = table_ref[0, p].astype(F32)
        to = table_ref[1, p]
        on = jnp.abs(sign)
        sr, si = spec[p, :, :SPAN], spec[p, :, SPAN:]
        spec_ref[to, :, :SPAN] = on * (sr * hr) - sign * (si * h_im)
        spec_ref[to, :, SPAN:] = on * (si * h_second) + sign * (sr * h_im)
    result = invert_right(spec_ref[...].reshape(slots * 32, PTS), inv_hi[...], inv_lo[...])
    out_ref[:, 0:32, :] = result.astype(BF16).reshape(slots, 32, SPAN)
    out_ref[:, 32:48, :] = (keep_ref[...] + other_ref[...].astype(F32)).astype(BF16)


def pair_taps_kernel(table_ref, got_ref, fwd_hi, fwd_lo, lag_hi, lag_lo, out_ref, spec_ref):
    slots = got_ref.shape[0]
    series = got_ref[:, 0:32, :].reshape(slots * 32, SPAN)
    spec_ref[...] = spectrum_right(series, fwd_hi[...], fwd_lo[...]).reshape(slots, 32, PTS)
    zero = lax.broadcasted_iota(jnp.int32, (32, SPAN), 1) == 0

    def step(p, carry):
        tr, ti = carry
        to = table_ref[1, p]
        on = jnp.where(table_ref[0, p] == 1, 1.0, 0.0)
        xs, gs = spec_ref[p], spec_ref[to]
        pr, pi = multiply(gs[:, :SPAN], gs[:, SPAN:], xs[:, :SPAN], xs[:, SPAN:], zero, -1.0)
        return tr + on * pr, ti + on * pi

    none = jnp.zeros((32, SPAN), F32)
    tr, ti = lax.fori_loop(0, slots, step, (none, none))
    out_ref[...] = invert_right(jnp.concatenate([tr, ti], 1), lag_hi[...], lag_lo[...])


def local_kernel(
    own_ref, other_ref, q_ref, k_ref, v_ref, c_ref, fwd_hi, fwd_lo, inv_hi, inv_lo,
    first_hi, first_lo, second_hi, second_lo, mixed_ref, series_ref,
):
    x = (k_ref[...].astype(F32) * v_ref[...].astype(F32)).astype(BF16)
    g = (c_ref[...].astype(F32) * q_ref[...].astype(F32)).astype(BF16)
    xs = spectrum_left(fwd_hi[...], fwd_lo[...], x)
    gs = spectrum_left(fwd_hi[...], fwd_lo[...], g)
    own, other = own_ref[...], other_ref[...]
    is_first = lax.axis_index("dp") == 0
    left = lax.broadcasted_iota(jnp.int32, own.shape, 2) < HALF

    def rows(packed):
        packed = packed.astype(F32)
        both = jnp.concatenate([jnp.where(left, packed, 0.0), jnp.where(left, 0.0, packed)], 1)
        return both.astype(BF16).reshape(own.shape[0] * 32, SPAN)

    first = rows(jnp.where(is_first, own.astype(F32), other.astype(F32)))
    second = rows(jnp.where(is_first, other.astype(F32), own.astype(F32)))
    nt = ((1,), (1,))
    hs = dot(first_hi[...], first, nt) + dot(first_lo[...], first, nt)
    hs = hs + (dot(second_hi[...], second, nt) + dot(second_lo[...], second, nt))
    zero = lax.broadcasted_iota(jnp.int32, (SPAN, x.shape[1]), 0) == 0
    hr, hi = hs[:SPAN], hs[SPAN:]
    mr, mi = multiply(xs[:SPAN], xs[SPAN:], hr, hi, zero, 1.0)
    mixed_ref[...] = invert_left(inv_hi[...], inv_lo[...], jnp.concatenate([mr, mi], 0))
    sr, si = multiply(gs[:SPAN], gs[SPAN:], hr, hi, zero, -1.0)
    series_ref[...] = invert_left(inv_hi[...], inv_lo[...], jnp.concatenate([sr, si], 0))


def tap_sum_kernel(got_ref, out_ref):
    out_ref[...] = jnp.sum(got_ref[...].astype(F32), axis=0)


def finish_kernel(
    slot_ref, len_ref, got_ref, mixed_ref, series_ref, k_ref, v_ref, c_ref,
    gq_ref, gk_ref, gv_ref,
):
    kind = own_kind(slot_ref, len_ref)
    rows = got_ref[:, 0:32, :].astype(F32).reshape(got_ref.shape[0] * 32, SPAN)
    pair = jnp.transpose(rows)
    mixed = mixed_ref[...] + jnp.where(kind == 2, pair, 0.0)
    series = series_ref[...] + jnp.where(kind == 1, pair, 0.0)
    mixed = mixed.astype(BF16).astype(F32)
    series = series.astype(BF16).astype(F32)
    gq_ref[...] = (c_ref[...].astype(F32) * mixed).astype(BF16)
    gk_ref[...] = (series * v_ref[...].astype(F32)).astype(BF16)
    gv_ref[...] = (series * k_ref[...].astype(F32)).astype(BF16)


def taps_out_kernel(scale, own_ref, other_ref, pair_ref, pair_other_ref, out_ref):
    is_first = lax.axis_index("dp") == 0
    own, other = own_ref[...], other_ref[...]
    first = jnp.where(is_first, own, other)
    second = jnp.where(is_first, other, own)
    lo, hi = pack_halves(first, second)
    near = jnp.concatenate([lo, hi], 0)
    total = pair_ref[...] + pair_other_ref[...]
    total = jnp.concatenate([total[:, :SPAN] + near, total[:, SPAN:]], 1)
    out_ref[...] = (jnp.transpose(total) * scale).astype(BF16)


SMEM = pl.BlockSpec(memory_space=pltpu.SMEM)
VMEM = pl.BlockSpec(memory_space=pltpu.VMEM)


def params():
    return pltpu.CompilerParams(vmem_limit_bytes=48 * 1024 * 1024)


def cost(flops, moved):
    return pl.CostEstimate(flops=int(flops), bytes_accessed=int(moved), transcendentals=0)


def per_device(query, key, value, cotangent, filter_taps, span_slot, doc_lengths):
    parts = lax.axis_size("ctx")
    tokens, width = query.shape
    scale = float(tokens * parts * lax.axis_size("dp")) ** (-0.5)
    forward, inverse = transforms()
    fwd = [jnp.asarray(m) for m in split_bf16(forward[:, :SPAN])]
    fwd_t = [jnp.asarray(m) for m in split_bf16(forward[:, :SPAN].T)]
    inv = [jnp.asarray(m) for m in split_bf16(inverse[:SPAN])]
    inv_t = [jnp.asarray(m) for m in split_bf16(inverse[:SPAN].T)]
    tap_t = [jnp.asarray(m) for m in split_bf16(np.roll(forward, -SPAN, 1).T)]
    lag_t = [jnp.asarray(m) for m in split_bf16(np.roll(inverse, SPAN, 0).T)]
    early, late = forward[:, :HALF], forward[:, HALF:SPAN]
    first = [jnp.asarray(m) for m in split_bf16(np.concatenate([early, early], 1))]
    second = [jnp.asarray(m) for m in split_bf16(np.concatenate([late, late], 1))]
    swap = [(0, 1), (1, 0)]
    block = 256
    steps = width // block
    wide = pl.BlockSpec((tokens, block), lambda i: (0, i))
    group = block // 32
    packed = pl.BlockSpec((group, 16, SPAN), lambda i: (i, 0, 0))

    def whole(array):
        return pl.BlockSpec(array.shape, lambda i: (0,) * array.ndim)

    out = pl.pallas_call(
        send_kernel,
        out_shape=jax.ShapeDtypeStruct((parts, 48, SPAN), BF16),
        in_specs=[SMEM, SMEM] + [VMEM] * 5,
        out_specs=VMEM,
        compiler_params=params(),
        cost_estimate=cost(2 * tokens * width, 10 * tokens * width),
        name="send",
    )(span_slot, doc_lengths, filter_taps, query, key, value, cotangent)
    got = lax.all_to_all(out, "ctx", split_axis=0, concat_axis=0, tiled=True)

    keep, give, table = pl.pallas_call(
        partial_kernel,
        grid=(steps,),
        out_shape=(
            jax.ShapeDtypeStruct((parts, 16, SPAN), F32),
            jax.ShapeDtypeStruct((parts, 16, SPAN), BF16),
            jax.ShapeDtypeStruct((2, parts), jnp.int32),
        ),
        in_specs=[SMEM, SMEM] + [wide] * 4 + [whole(m) for m in fwd + inv],
        out_specs=(packed, packed, SMEM),
        scratch_shapes=[pltpu.SMEM((parts,), jnp.int32)],
        compiler_params=params(),
        cost_estimate=cost(2e9, 10 * tokens * width),
        name="partial_taps",
    )(span_slot, doc_lengths, query, key, value, cotangent, *fwd, *inv)
    taken = lax.ppermute(give, "dp", swap)

    back = pl.pallas_call(
        pair_kernel,
        out_shape=jax.ShapeDtypeStruct((parts, 48, SPAN), BF16),
        in_specs=[SMEM] + [VMEM] * 10,
        out_specs=VMEM,
        scratch_shapes=[pltpu.VMEM((parts, 32, PTS), F32)],
        compiler_params=params(),
        cost_estimate=cost(1e9, 10 * tokens * width),
        name="pair",
    )(table, got, filter_taps, keep, taken, *fwd_t, *inv_t, *tap_t)
    landed = lax.all_to_all(back, "ctx", split_axis=0, concat_axis=0, tiled=True)

    pair_taps = pl.pallas_call(
        pair_taps_kernel,
        out_shape=jax.ShapeDtypeStruct((32, PTS), F32),
        in_specs=[SMEM] + [VMEM] * 5,
        out_specs=VMEM,
        scratch_shapes=[pltpu.VMEM((parts, 32, PTS), F32)],
        compiler_params=params(),
        cost_estimate=cost(1e9, 6 * tokens * width),
        name="pair_taps",
    )(table, got, *fwd_t, *lag_t)
    pair_taps_other = lax.ppermute(pair_taps, "dp", swap)

    taps_own = got[:, 32:48, :]
    taps_other = lax.ppermute(taps_own, "dp", swap)
    mixed, series = pl.pallas_call(
        local_kernel,
        grid=(steps,),
        out_shape=(jax.ShapeDtypeStruct((tokens, width), F32),) * 2,
        in_specs=[packed, packed] + [wide] * 4 + [whole(m) for m in fwd + inv + first + second],
        out_specs=(wide, wide),
        compiler_params=params(),
        cost_estimate=cost(3e9, 20 * tokens * width),
        name="local",
    )(taps_own, taps_other, query, key, value, cotangent, *fwd, *inv, *first, *second)

    near = pl.pallas_call(
        tap_sum_kernel,
        grid=(1,),
        out_shape=jax.ShapeDtypeStruct((16, SPAN), F32),
        in_specs=[pl.BlockSpec((parts, 16, SPAN), lambda i: (0, 2, 0))],
        out_specs=pl.BlockSpec((16, SPAN), lambda i: (0, 0)),
        compiler_params=params(),
        cost_estimate=cost(parts * 16 * SPAN, parts * 32 * SPAN),
        name="tap_sum",
    )(landed)
    near_other = lax.ppermute(near, "dp", swap)

    grads = pl.pallas_call(
        finish_kernel,
        grid=(steps,),
        out_shape=(jax.ShapeDtypeStruct((tokens, width), BF16),) * 3,
        in_specs=[SMEM, SMEM, pl.BlockSpec((group, 48, SPAN), lambda i: (i, 0, 0))] + [wide] * 5,
        out_specs=(wide,) * 3,
        compiler_params=params(),
        cost_estimate=cost(10 * tokens * width, 24 * tokens * width),
        name="finish",
    )(span_slot, doc_lengths, landed, mixed, series, key, value, cotangent)

    grad_filter = pl.pallas_call(
        functools.partial(taps_out_kernel, scale),
        out_shape=jax.ShapeDtypeStruct((PTS, 32), BF16),
        in_specs=[VMEM] * 4,
        out_specs=VMEM,
        compiler_params=params(),
        name="taps_out",
    )(near, near_other, pair_taps, pair_taps_other)
    return (*grads, grad_filter)


def solution(mesh):
    return jax.shard_map(
        per_device,
        mesh=mesh,
        in_specs=(
            P(("dp", "ctx"), "ch"),
            P(("dp", "ctx"), "ch"),
            P(("dp", "ctx"), "ch"),
            P(("dp", "ctx"), "ch"),
            P(None, ("ch", "ctx")),
            P("dp", None),
            P("dp", None),
        ),
        out_specs=(
            P(("dp", "ctx"), "ch"),
            P(("dp", "ctx"), "ch"),
            P(("dp", "ctx"), "ch"),
            P(None, ("ch", "ctx")),
        ),
        check_vma=False,
    )
```

```python
import functools

import jax
import jax.numpy as jnp
import numpy as np
from jax import lax
from jax.experimental import pallas as pl
from jax.experimental.pallas import tpu as pltpu
from jax.sharding import PartitionSpec as P

SPAN = 128
PTS = 2 * SPAN
QUARTER = SPAN // 4
F32, BF16 = jnp.float32, jnp.bfloat16


def split_bf16(matrix):
    high = matrix.astype(BF16)
    low = (matrix - high.astype(np.float64)).astype(BF16)
    return high, low


def transforms():
    freq = np.arange(SPAN)[:, None]
    point = np.arange(PTS)[None, :]
    angle = 2 * np.pi * ((freq * point) % PTS) / PTS
    real, imag = np.cos(angle), -np.sin(angle)
    imag[0] = np.where(np.arange(PTS) % 2 == 0, 1.0, -1.0)
    forward = np.concatenate([real, imag], 0)
    weight = np.full((PTS, 1), 2.0 / PTS)
    weight[0], weight[SPAN] = 1.0 / PTS, 1.0 / PTS
    inverse = (forward * weight).T
    return forward, inverse


def dot(a, b, dims=((1,), (0,))):
    return lax.dot_general(a, b, (dims, ((), ())), preferred_element_type=F32)


def halves(x):
    high = x.astype(BF16)
    return high, (x - high.astype(F32)).astype(BF16)


def spectrum_left(high, low, x):
    return dot(high, x) + dot(low, x)


def spectrum_right(x, high, low):
    return dot(x, high) + dot(x, low)


def invert_left(high, low, spec):
    s_high, s_low = halves(spec)
    return dot(high, s_high) + (dot(high, s_low) + dot(low, s_high))


def invert_right(spec, high, low):
    s_high, s_low = halves(spec)
    return dot(s_high, high) + (dot(s_low, high) + dot(s_high, low))


def multiply(ar, ai, br, bi, zero, sign):
    b_im = sign * jnp.where(zero, 0.0, bi)
    b_second = jnp.where(zero, bi, br)
    return ar * br - ai * b_im, ai * b_second + ar * b_im


def swap_blocks(parts):
    axis = parts[0].ndim - 1
    block = lax.broadcasted_iota(jnp.int32, parts[0].shape, axis) // QUARTER
    result = []
    for t in range(4):
        total = parts[t]
        for b in range(4):
            if b != t:
                moved = pltpu.roll(parts[b], (QUARTER * (b - t)) % SPAN, axis)
                total = jnp.where(block == b, moved, total)
        result.append(total)
    return result


def own_kind(slot_ref, len_ref):
    span = slot_ref[0, lax.axis_index("ctx")]

    def step(d, carry):
        pos, kind = carry
        length = len_ref[0, d]
        two = length == 2
        kind = jnp.where(two & (span == pos), 1, kind)
        kind = jnp.where(two & (span == pos + 1), 2, kind)
        return pos + length, kind

    zero = jnp.int32(0)
    return lax.fori_loop(0, len_ref.shape[1], step, (zero, zero))[1]


def send_kernel(
    slot_hbm, len_hbm, taps_hbm, q_hbm, k_hbm, v_hbm, c_hbm, out_hbm,
    slot_ref, len_ref, taps_ref, q_buf, k_buf, v_buf, c_buf, out_buf,
    small_sem, in_sem, out_sem,
):
    chunks = out_sem.shape[0]
    width = q_buf.shape[1] // chunks
    count = out_buf.shape[0] // chunks
    small = [
        pltpu.make_async_copy(src, dst, small_sem.at[i])
        for i, (src, dst) in enumerate(
            ((slot_hbm, slot_ref), (len_hbm, len_ref), (taps_hbm, taps_ref))
        )
    ]
    small[0].start()
    small[1].start()
    wide = []
    for j in range(chunks):
        cols = pl.ds(j * width, width)
        wide.append([
            pltpu.make_async_copy(src.at[:, cols], dst.at[:, cols], in_sem.at[i, j])
            for i, (src, dst) in enumerate(
                ((k_hbm, k_buf), (v_hbm, v_buf), (c_hbm, c_buf), (q_hbm, q_buf))
            )
        ])
        for copy in wide[-1]:
            copy.start()
        if j == 0:
            small[2].start()
    small[0].wait()
    small[1].wait()
    first = own_kind(slot_ref, len_ref) == 1
    small[2].wait()
    taps = taps_ref[:, 0:SPAN].astype(F32)
    quarters = swap_blocks([taps[8 * b:8 * b + 8] for b in range(4)])
    core = lax.axis_index("dp") == 0
    outs = []
    for j in range(chunks):
        for copy in wide[j]:
            copy.wait()
        cols = slice(j * width, (j + 1) * width)
        rows = slice(j * count, (j + 1) * count)
        a = jnp.where(first, k_buf[:, cols].astype(F32), c_buf[:, cols].astype(F32))
        b = jnp.where(first, v_buf[:, cols].astype(F32), q_buf[:, cols].astype(F32))
        out_buf[rows, 0:32, :] = jnp.transpose((a * b).astype(BF16)).reshape(count, 32, SPAN)
        far = int(2 * j >= chunks)
        mine = jnp.where(core, quarters[far], quarters[2 + far]).astype(BF16)
        out_buf[rows, 32:40, :] = jnp.broadcast_to(mine[None], (count, 8, SPAN))
        out = pltpu.make_async_copy(out_buf.at[rows], out_hbm.at[rows], out_sem.at[j])
        out.start()
        outs.append(out)
    for out in outs:
        out.wait()


def partial_kernel(
    slot_ref, len_ref, q_ref, k_ref, v_ref, c_ref, fwd_hi, fwd_lo, inv_hi, inv_lo,
    keep_ref, give_ref, table_ref, inverse_ref,
):
    @pl.when(pl.program_id(0) == 0)
    def _():
        slots = slot_ref.shape[1]

        def fill(r, carry):
            inverse_ref[slot_ref[0, r]] = r
            return carry

        lax.fori_loop(0, slots, fill, 0)

        def step(d, carry):
            pos, count = carry
            length = len_ref[0, d]

            @pl.when(length == 2)
            def _():
                table_ref[0, count] = inverse_ref[pos]
                table_ref[1, count] = inverse_ref[pos + 1]

            return pos + length, count + length - 1

        lax.fori_loop(0, len_ref.shape[1], step, (jnp.int32(0), jnp.int32(0)))
        table_ref[2, 0] = own_kind(slot_ref, len_ref)

    x = (k_ref[...].astype(F32) * v_ref[...].astype(F32)).astype(BF16)
    g = (c_ref[...].astype(F32) * q_ref[...].astype(F32)).astype(BF16)
    xs = spectrum_left(fwd_hi[...], fwd_lo[...], x)
    gs = spectrum_left(fwd_hi[...], fwd_lo[...], g)
    zero = lax.broadcasted_iota(jnp.int32, (SPAN, x.shape[1]), 0) == 0
    pr, pi = multiply(gs[:SPAN], gs[SPAN:], xs[:SPAN], xs[SPAN:], zero, -1.0)
    taps = invert_left(inv_hi[...], inv_lo[...], jnp.concatenate([pr, pi], 0))
    count = x.shape[1] // 32
    rows = jnp.transpose(taps).reshape(count, 4, 8, SPAN)
    quarters = swap_blocks([rows[:, b] for b in range(4)])
    core = lax.axis_index("dp") == 0
    for t in range(2):
        low = quarters[t].reshape(count * 8, SPAN)
        high = quarters[2 + t].reshape(count * 8, SPAN)
        keep_ref[t] = jnp.where(core, low, high)
        give_ref[t] = jnp.where(core, high, low).astype(BF16)


def halve_kernel(own_ref, other_ref, keep_ref, give_ref):
    far = lax.axis_index("ctx") // 16 == 1
    low = own_ref[0] + other_ref[0].astype(F32)
    high = own_ref[1] + other_ref[1].astype(F32)
    keep_ref[...] = jnp.where(far, high, low)
    give_ref[...] = jnp.where(far, low, high).astype(BF16)


def pair_spectra(table_ref, got_ref, fwd_hi, fwd_lo):
    pairs = table_ref.shape[1]
    rows = [got_ref[table_ref[k, p], 0:32, :] for k in range(2) for p in range(pairs)]
    spec = spectrum_right(jnp.concatenate(rows, 0), fwd_hi[...], fwd_lo[...])
    return spec.reshape(2, pairs, 32, PTS)


def pair_kernel(
    table_ref, got_ref, taps_ref, keep_ref, other_ref, fwd_hi, fwd_lo, inv_hi, inv_lo,
    tap_hi, tap_lo, out_ref,
):
    slots, pairs = got_ref.shape[0], table_ref.shape[1]
    hs = spectrum_right(taps_ref[...], tap_hi[...], tap_lo[...])
    hr, hi = hs[:, :SPAN], hs[:, SPAN:]
    zero = lax.broadcasted_iota(jnp.int32, hr.shape, 1) == 0
    spec = pair_spectra(table_ref, got_ref, fwd_hi, fwd_lo)
    out_ref[:, 0:32, :] = jnp.zeros((slots, 32, SPAN), BF16)
    for k in range(2):
        sr, si = spec[k, :, :, :SPAN], spec[k, :, :, SPAN:]
        pr, pi = multiply(sr, si, hr[None], hi[None], zero[None], 1.0 if k == 0 else -1.0)
        both = jnp.concatenate([pr, pi], 2).reshape(pairs * 32, PTS)
        result = invert_right(both, inv_hi[...], inv_lo[...]).astype(BF16)
        for p in range(pairs):
            out_ref[table_ref[1 - k, p], 0:32, :] = result[32 * p:32 * p + 32]
    near = (keep_ref[...] + other_ref[...].astype(F32)).astype(BF16)
    out_ref[:, 32:40, :] = near.reshape(slots, 8, SPAN)


def pair_taps_kernel(table_ref, got_ref, fwd_hi, fwd_lo, lag_hi, lag_lo, out_ref):
    spec = pair_spectra(table_ref, got_ref, fwd_hi, fwd_lo)
    zero = lax.broadcasted_iota(jnp.int32, (1, 32, SPAN), 2) == 0
    xs, gs = spec[0], spec[1]
    tr, ti = multiply(
        gs[:, :, :SPAN], gs[:, :, SPAN:], xs[:, :, :SPAN], xs[:, :, SPAN:], zero, -1.0
    )
    both = jnp.concatenate([jnp.sum(tr, 0), jnp.sum(ti, 0)], 1)
    out_ref[...] = invert_right(both, lag_hi[...], lag_lo[...])


def local_kernel(
    own_ref, side_ref, core_ref, core_side_ref, q_ref, k_ref, v_ref, c_ref,
    fwd_hi, fwd_lo, inv_hi, inv_lo, taps_hi, taps_lo, mixed_ref, series_ref,
):
    x = (k_ref[...].astype(F32) * v_ref[...].astype(F32)).astype(BF16)
    g = (c_ref[...].astype(F32) * q_ref[...].astype(F32)).astype(BF16)
    xs = spectrum_left(fwd_hi[...], fwd_lo[...], x)
    gs = spectrum_left(fwd_hi[...], fwd_lo[...], g)
    count = own_ref.shape[0] // 8
    dp, far = lax.axis_index("dp"), lax.axis_index("ctx") // 16
    own, side = own_ref[...].astype(F32), side_ref[...].astype(F32)
    core, core_side = core_ref[0].astype(F32), core_side_ref[0].astype(F32)
    quarters = []
    for t in range(4):
        same = jnp.where(far == t % 2, own, side)
        cross = jnp.where(far == t % 2, core, core_side)
        quarters.append(jnp.where(dp == t // 2, same, cross).reshape(count, 8, SPAN))
    taps = jnp.concatenate(swap_blocks(quarters), 1).reshape(count * 32, SPAN).astype(BF16)
    nt = ((1,), (1,))
    hs = dot(taps_hi[...], taps, nt) + dot(taps_lo[...], taps, nt)
    zero = lax.broadcasted_iota(jnp.int32, (SPAN, x.shape[1]), 0) == 0
    hr, hi = hs[:SPAN], hs[SPAN:]
    mr, mi = multiply(xs[:SPAN], xs[SPAN:], hr, hi, zero, 1.0)
    mixed_ref[...] = invert_left(inv_hi[...], inv_lo[...], jnp.concatenate([mr, mi], 0))
    sr, si = multiply(gs[:SPAN], gs[SPAN:], hr, hi, zero, -1.0)
    series_ref[...] = invert_left(inv_hi[...], inv_lo[...], jnp.concatenate([sr, si], 0))


def taps_kernel(got_ref, pair_ref, after_ref, out_ref):
    del after_ref
    slots = got_ref.shape[0]
    core = lax.axis_index("dp")
    sums = []
    for far in range(2):
        rows = got_ref[far * 16:far * 16 + 16, 32:40, :].astype(F32)
        sums.append(jnp.sum(rows, axis=0))
    quarters = [jnp.where(core == t // 2, sums[t % 2], 0.0) for t in range(4)]
    near = jnp.concatenate(swap_blocks(quarters), 0)
    out_ref[:, :SPAN] = pair_ref[:, :SPAN] + near
    out_ref[:, SPAN:] = pair_ref[:, SPAN:]


def finish_kernel(
    table_ref, got_ref, mixed_ref, series_ref, k_ref, v_ref, c_ref,
    gq_ref, gk_ref, gv_ref, q_buf, k_buf, v_buf, sems,
):
    chunks = sems.shape[1]
    width = q_buf.shape[1] // chunks
    count = got_ref.shape[0] // chunks
    kind = table_ref[2, 0]
    copies = []
    for j in range(chunks):
        cols = slice(j * width, (j + 1) * width)
        rows = got_ref[j * count:(j + 1) * count, 0:32, :].reshape(width, SPAN)
        pair = jnp.transpose(rows).astype(F32)
        mixed = mixed_ref[:, cols] + jnp.where(kind == 2, pair, 0.0)
        series = series_ref[:, cols] + jnp.where(kind == 1, pair, 0.0)
        mixed = mixed.astype(BF16).astype(F32)
        series = series.astype(BF16).astype(F32)
        q_buf[:, cols] = (c_ref[:, cols].astype(F32) * mixed).astype(BF16)
        k_buf[:, cols] = (series * v_ref[:, cols].astype(F32)).astype(BF16)
        v_buf[:, cols] = (series * k_ref[:, cols].astype(F32)).astype(BF16)
        for i, (buf, ref) in enumerate(((q_buf, gq_ref), (k_buf, gk_ref), (v_buf, gv_ref))):
            copy = pltpu.make_async_copy(buf.at[:, cols], ref.at[:, cols], sems.at[i, j])
            copy.start()
            copies.append(copy)
    for copy in copies:
        copy.wait()


def taps_out_kernel(scale, own_ref, other_ref, out_ref):
    out_ref[...] = ((own_ref[...] + other_ref[...]) * scale).astype(BF16)


SMEM = pl.BlockSpec(memory_space=pltpu.SMEM)
VMEM = pl.BlockSpec(memory_space=pltpu.VMEM)
HBM = pl.BlockSpec(memory_space=pltpu.HBM)
ANY = pl.BlockSpec(memory_space=pl.ANY)
DMA = pltpu.SemaphoreType.DMA


def params(mebibytes=32):
    return pltpu.CompilerParams(vmem_limit_bytes=mebibytes * 1024 * 1024)


def cost(flops, moved):
    return pl.CostEstimate(flops=int(flops), bytes_accessed=int(moved), transcendentals=0)


def per_device(query, key, value, cotangent, filter_taps, span_slot, doc_lengths):
    parts = lax.axis_size("ctx")
    tokens, width = query.shape
    area = tokens * width
    pairs = parts - doc_lengths.shape[1]
    scale = float(tokens * parts * lax.axis_size("dp")) ** (-0.5)
    forward, inverse = transforms()

    def constant(matrix):
        return [jnp.asarray(m) for m in split_bf16(matrix)]

    fwd = constant(forward[:, :SPAN])
    fwd_t = constant(forward[:, :SPAN].T)
    inv = constant(inverse[:SPAN])
    inv_t = constant(inverse[:SPAN].T)
    tap_t = constant(np.roll(forward, -SPAN, 1).T)
    lag_t = constant(np.roll(inverse, SPAN, 0).T)
    core_swap = [(0, 1), (1, 0)]
    side_swap = [(c, c ^ 16) for c in range(parts)]
    block = 256
    steps = width // block
    group = block // 32
    wide = pl.BlockSpec((tokens, block), lambda i: (0, i))
    taps_rows = filter_taps.T

    def whole(array):
        return pl.BlockSpec(array.shape, lambda i: (0,) * array.ndim)

    chunk = jax.ShapeDtypeStruct((parts, 40, SPAN), BF16)
    out = pl.pallas_call(
        send_kernel,
        out_shape=chunk,
        in_specs=[HBM] * 7,
        out_specs=HBM,
        scratch_shapes=[
            pltpu.SMEM(span_slot.shape, jnp.int32),
            pltpu.SMEM(doc_lengths.shape, jnp.int32),
            pltpu.VMEM(taps_rows.shape, BF16),
        ] + [pltpu.VMEM((tokens, width), BF16)] * 4 + [
            pltpu.VMEM(chunk.shape, BF16), DMA((3,)), DMA((4, steps)), DMA((steps,)),
        ],
        compiler_params=params(60),
        cost_estimate=cost(2 * area, 8 * area),
        name="send",
    )(span_slot, doc_lengths, taps_rows, query, key, value, cotangent)
    got = lax.all_to_all(out, "ctx", split_axis=0, concat_axis=0, tiled=True)

    two = pl.BlockSpec((2, group * 8, SPAN), lambda i: (0, i, 0))
    keep, give, table = pl.pallas_call(
        partial_kernel,
        grid=(steps,),
        out_shape=(
            jax.ShapeDtypeStruct((2, parts * 8, SPAN), F32),
            jax.ShapeDtypeStruct((2, parts * 8, SPAN), BF16),
            jax.ShapeDtypeStruct((3, pairs), jnp.int32),
        ),
        in_specs=[SMEM, SMEM] + [wide] * 4 + [whole(m) for m in fwd + inv],
        out_specs=(two, two, SMEM),
        scratch_shapes=[pltpu.SMEM((parts,), jnp.int32)],
        compiler_params=params(),
        cost_estimate=cost(2e9, 10 * area),
        name="partial_taps",
    )(span_slot, doc_lengths, query, key, value, cotangent, *fwd, *inv)
    taken = lax.ppermute(give, "dp", core_swap)

    keep, give = pl.pallas_call(
        halve_kernel,
        out_shape=(
            jax.ShapeDtypeStruct((parts * 8, SPAN), F32),
            jax.ShapeDtypeStruct((parts * 8, SPAN), BF16),
        ),
        in_specs=[VMEM, VMEM],
        out_specs=(VMEM, VMEM),
        compiler_params=params(),
        cost_estimate=cost(area, 3 * area),
        name="halve",
    )(keep, taken)
    near_other = lax.ppermute(give, "ctx", side_swap)

    back = pl.pallas_call(
        pair_kernel,
        out_shape=chunk,
        in_specs=[SMEM] + [VMEM] * 10,
        out_specs=VMEM,
        compiler_params=params(),
        cost_estimate=cost(1e9, 8 * area),
        name="pair",
    )(table, got, taps_rows, keep, near_other, *fwd_t, *inv_t, *tap_t)
    landed = lax.all_to_all(back, "ctx", split_axis=0, concat_axis=0, tiled=True)

    own = got[:, 32:40, :].reshape(parts * 8, SPAN)
    side = lax.ppermute(own, "ctx", side_swap)
    core = lax.ppermute(jnp.stack([own, side]), "dp", core_swap)
    quarter = pl.BlockSpec((group * 8, SPAN), lambda i: (i, 0))
    mixed, series = pl.pallas_call(
        local_kernel,
        grid=(steps,),
        out_shape=(jax.ShapeDtypeStruct((tokens, width), F32),) * 2,
        in_specs=[
            quarter, quarter,
            pl.BlockSpec((1, group * 8, SPAN), lambda i: (0, i, 0)),
            pl.BlockSpec((1, group * 8, SPAN), lambda i: (1, i, 0)),
        ] + [wide] * 4 + [whole(m) for m in fwd + inv + fwd],
        out_specs=(wide, wide),
        compiler_params=params(),
        cost_estimate=cost(3e9, 20 * area),
        name="local",
    )(own, side, core, core, query, key, value, cotangent, *fwd, *inv, *fwd)

    pair_taps = pl.pallas_call(
        pair_taps_kernel,
        out_shape=jax.ShapeDtypeStruct((32, PTS), F32),
        in_specs=[SMEM] + [VMEM] * 5,
        out_specs=VMEM,
        compiler_params=params(),
        cost_estimate=cost(1e9, 6 * area),
        name="pair_taps",
    )(table, got, *fwd_t, *lag_t)
    taps_own = pl.pallas_call(
        taps_kernel,
        out_shape=jax.ShapeDtypeStruct((32, PTS), F32),
        in_specs=[VMEM, VMEM, ANY],
        out_specs=VMEM,
        compiler_params=params(),
        cost_estimate=cost(area, area),
        name="taps",
    )(landed, pair_taps, mixed)
    taps_other = lax.ppermute(taps_own, "dp", core_swap)

    result = jax.ShapeDtypeStruct((tokens, width), BF16)
    grads = pl.pallas_call(
        finish_kernel,
        out_shape=(result,) * 3,
        in_specs=[SMEM] + [VMEM] * 6,
        out_specs=(HBM,) * 3,
        scratch_shapes=[pltpu.VMEM((tokens, width), BF16)] * 3 + [DMA((3, steps))],
        compiler_params=params(),
        cost_estimate=cost(10 * area, 20 * area),
        name="finish",
    )(table, landed, mixed, series, key, value, cotangent)
    grad_filter = pl.pallas_call(
        functools.partial(taps_out_kernel, scale),
        out_shape=jax.ShapeDtypeStruct((32, PTS), BF16),
        in_specs=[VMEM] * 2,
        out_specs=VMEM,
        compiler_params=params(),
        name="taps_out",
    )(taps_own, taps_other)
    return (*grads, grad_filter.T)


def solution(mesh):
    return jax.shard_map(
        per_device,
        mesh=mesh,
        in_specs=(
            P(("dp", "ctx"), "ch"),
            P(("dp", "ctx"), "ch"),
            P(("dp", "ctx"), "ch"),
            P(("dp", "ctx"), "ch"),
            P(None, ("ch", "ctx")),
            P("dp", None),
            P("dp", None),
        ),
        out_specs=(
            P(("dp", "ctx"), "ch"),
            P(("dp", "ctx"), "ch"),
            P(("dp", "ctx"), "ch"),
            P(None, ("ch", "ctx")),
        ),
        check_vma=False,
    )
```

```python
import functools

import jax
import jax.numpy as jnp
import numpy as np
from jax import lax
from jax.experimental import pallas as pl
from jax.experimental.pallas import tpu as pltpu
from jax.sharding import PartitionSpec as P

SPAN = 128
PTS = 2 * SPAN
QUARTER = SPAN // 4
TURN = 24
TURN_BLOCK = TURN // 8
F32, BF16 = jnp.float32, jnp.bfloat16


def split_bf16(matrix):
    high = matrix.astype(BF16)
    low = (matrix - high.astype(np.float64)).astype(BF16)
    return high, low


def transforms():
    freq = np.arange(SPAN)[:, None]
    point = np.arange(PTS)[None, :]
    angle = 2 * np.pi * ((freq * point) % PTS) / PTS
    real, imag = np.cos(angle), -np.sin(angle)
    imag[0] = np.where(np.arange(PTS) % 2 == 0, 1.0, -1.0)
    forward = np.concatenate([real, imag], 0)
    weight = np.full((PTS, 1), 2.0 / PTS)
    weight[0], weight[SPAN] = 1.0 / PTS, 1.0 / PTS
    inverse = (forward * weight).T
    return forward, inverse


def dot(a, b, dims=((1,), (0,))):
    return lax.dot_general(a, b, (dims, ((), ())), preferred_element_type=F32)


def halves(x):
    high = x.astype(BF16)
    return high, (x - high.astype(F32)).astype(BF16)


def spectrum_left(high, low, x):
    return dot(high, x) + dot(low, x)


def spectrum_right(x, high, low):
    return dot(x, high) + dot(x, low)


def invert_left(high, low, spec):
    s_high, s_low = halves(spec)
    return dot(high, s_high) + (dot(high, s_low) + dot(low, s_high))


def invert_right(spec, high, low):
    s_high, s_low = halves(spec)
    return dot(s_high, high) + (dot(s_low, high) + dot(s_high, low))


def multiply(ar, ai, br, bi, zero, sign):
    b_im = sign * jnp.where(zero, 0.0, bi)
    b_second = jnp.where(zero, bi, br)
    return ar * br - ai * b_im, ai * b_second + ar * b_im


def swap_blocks(parts):
    axis = parts[0].ndim - 1
    block = lax.broadcasted_iota(jnp.int32, parts[0].shape, axis) // QUARTER
    result = []
    for t in range(4):
        total = parts[t]
        for b in range(4):
            if b != t:
                moved = pltpu.roll(parts[b], (QUARTER * (b - t)) % SPAN, axis)
                total = jnp.where(block == b, moved, total)
        result.append(total)
    return result


def own_kind(slot_ref, len_ref):
    span = slot_ref[0, lax.axis_index("ctx")]

    def step(d, carry):
        pos, kind = carry
        length = len_ref[0, d]
        two = length == 2
        kind = jnp.where(two & (span == pos), 1, kind)
        kind = jnp.where(two & (span == pos + 1), 2, kind)
        return pos + length, kind

    zero = jnp.int32(0)
    return lax.fori_loop(0, len_ref.shape[1], step, (zero, zero))[1]


def send_kernel(
    slot_hbm, len_hbm, taps_hbm, q_hbm, k_hbm, v_hbm, c_hbm, out_hbm,
    slot_ref, len_ref, taps_ref, q_buf, k_buf, v_buf, c_buf, out_buf,
    small_sem, in_sem, out_sem,
):
    chunks = out_sem.shape[0]
    width = q_buf.shape[1] // chunks
    count = out_buf.shape[0] // chunks
    small = [
        pltpu.make_async_copy(src, dst, small_sem.at[i])
        for i, (src, dst) in enumerate(
            ((slot_hbm, slot_ref), (len_hbm, len_ref), (taps_hbm, taps_ref))
        )
    ]
    small[0].start()
    small[1].start()
    wide = []
    for j in range(chunks):
        cols = pl.ds(j * width, width)
        wide.append([
            pltpu.make_async_copy(src.at[:, cols], dst.at[:, cols], in_sem.at[i, j])
            for i, (src, dst) in enumerate(
                ((k_hbm, k_buf), (v_hbm, v_buf), (c_hbm, c_buf), (q_hbm, q_buf))
            )
        ])
        for copy in wide[-1]:
            copy.start()
        if j == 0:
            small[2].start()
    small[0].wait()
    small[1].wait()
    first = own_kind(slot_ref, len_ref) == 1
    small[2].wait()
    taps = taps_ref[:, 0:SPAN].astype(F32)
    quarters = swap_blocks([taps[8 * b:8 * b + 8] for b in range(4)])
    core = lax.axis_index("dp") == 0
    outs = []
    for j in range(chunks):
        for copy in wide[j]:
            copy.wait()
        cols = slice(j * width, (j + 1) * width)
        place = j ^ TURN_BLOCK
        rows = slice(place * count, (place + 1) * count)
        a = jnp.where(first, k_buf[:, cols].astype(F32), c_buf[:, cols].astype(F32))
        b = jnp.where(first, v_buf[:, cols].astype(F32), q_buf[:, cols].astype(F32))
        out_buf[rows, 0:32, :] = jnp.transpose((a * b).astype(BF16)).reshape(count, 32, SPAN)
        far = int(2 * j >= chunks)
        mine = jnp.where(core, quarters[far], quarters[2 + far]).astype(BF16)
        out_buf[rows, 32:40, :] = jnp.broadcast_to(mine[None], (count, 8, SPAN))
        out = pltpu.make_async_copy(out_buf.at[rows], out_hbm.at[rows], out_sem.at[j])
        out.start()
        outs.append(out)
    for out in outs:
        out.wait()


def partial_kernel(
    slot_ref, len_ref, q_ref, k_ref, v_ref, c_ref, fwd_hi, fwd_lo, inv_hi, inv_lo,
    keep_ref, give_ref, table_ref, inverse_ref,
):
    @pl.when(pl.program_id(0) == 0)
    def _():
        slots = slot_ref.shape[1]

        def fill(r, carry):
            inverse_ref[slot_ref[0, r]] = r
            return carry

        lax.fori_loop(0, slots, fill, 0)

        def step(d, carry):
            pos, count = carry
            length = len_ref[0, d]

            @pl.when(length == 2)
            def _():
                table_ref[0, count] = inverse_ref[pos]
                table_ref[1, count] = inverse_ref[pos + 1]

            return pos + length, count + length - 1

        lax.fori_loop(0, len_ref.shape[1], step, (jnp.int32(0), jnp.int32(0)))
        table_ref[2, 0] = own_kind(slot_ref, len_ref)

    x = (k_ref[...].astype(F32) * v_ref[...].astype(F32)).astype(BF16)
    g = (c_ref[...].astype(F32) * q_ref[...].astype(F32)).astype(BF16)
    xs = spectrum_left(fwd_hi[...], fwd_lo[...], x)
    gs = spectrum_left(fwd_hi[...], fwd_lo[...], g)
    zero = lax.broadcasted_iota(jnp.int32, (SPAN, x.shape[1]), 0) == 0
    pr, pi = multiply(gs[:SPAN], gs[SPAN:], xs[:SPAN], xs[SPAN:], zero, -1.0)
    taps = invert_left(inv_hi[...], inv_lo[...], jnp.concatenate([pr, pi], 0))
    count = x.shape[1] // 32
    rows = jnp.transpose(taps).reshape(count, 4, 8, SPAN)
    quarters = swap_blocks([rows[:, b] for b in range(4)])
    core = lax.axis_index("dp") == 0
    for t in range(2):
        low = quarters[t].reshape(count * 8, SPAN)
        high = quarters[2 + t].reshape(count * 8, SPAN)
        keep_ref[t] = jnp.where(core, low, high)
        give_ref[t] = jnp.where(core, high, low).astype(BF16)


def halve_kernel(own_ref, other_ref, keep_ref, give_ref):
    far = lax.axis_index("ctx") // 16 == 1
    low = own_ref[0] + other_ref[0].astype(F32)
    high = own_ref[1] + other_ref[1].astype(F32)
    keep_ref[...] = jnp.where(far, high, low)
    give_ref[...] = jnp.where(far, low, high).astype(BF16)


def pair_spectra(table_ref, got_ref, fwd_hi, fwd_lo):
    pairs = table_ref.shape[1]
    rows = [got_ref[table_ref[k, p] ^ TURN, 0:32, :] for k in range(2) for p in range(pairs)]
    spec = spectrum_right(jnp.concatenate(rows, 0), fwd_hi[...], fwd_lo[...])
    return spec.reshape(2, pairs, 32, PTS)


def pair_kernel(
    table_ref, got_ref, taps_ref, keep_ref, other_ref, fwd_hi, fwd_lo, inv_hi, inv_lo,
    tap_hi, tap_lo, out_ref,
):
    slots, pairs = got_ref.shape[0], table_ref.shape[1]
    hs = spectrum_right(taps_ref[...], tap_hi[...], tap_lo[...])
    hr, hi = hs[:, :SPAN], hs[:, SPAN:]
    zero = lax.broadcasted_iota(jnp.int32, hr.shape, 1) == 0
    spec = pair_spectra(table_ref, got_ref, fwd_hi, fwd_lo)
    out_ref[:, 0:32, :] = jnp.zeros((slots, 32, SPAN), BF16)
    for k in range(2):
        sr, si = spec[k, :, :, :SPAN], spec[k, :, :, SPAN:]
        pr, pi = multiply(sr, si, hr[None], hi[None], zero[None], 1.0 if k == 0 else -1.0)
        both = jnp.concatenate([pr, pi], 2).reshape(pairs * 32, PTS)
        result = invert_right(both, inv_hi[...], inv_lo[...]).astype(BF16)
        for p in range(pairs):
            out_ref[table_ref[1 - k, p] ^ TURN, 0:32, :] = result[32 * p:32 * p + 32]
    near = (keep_ref[...] + other_ref[...].astype(F32)).astype(BF16)
    near = near.reshape(slots, 8, SPAN)
    for j in range(slots // 8):
        place = 8 * (j ^ TURN_BLOCK)
        out_ref[place:place + 8, 32:40, :] = near[8 * j:8 * j + 8]


def pair_taps_kernel(table_ref, got_ref, fwd_hi, fwd_lo, lag_hi, lag_lo, out_ref):
    spec = pair_spectra(table_ref, got_ref, fwd_hi, fwd_lo)
    zero = lax.broadcasted_iota(jnp.int32, (1, 32, SPAN), 2) == 0
    xs, gs = spec[0], spec[1]
    tr, ti = multiply(
        gs[:, :, :SPAN], gs[:, :, SPAN:], xs[:, :, :SPAN], xs[:, :, SPAN:], zero, -1.0
    )
    both = jnp.concatenate([jnp.sum(tr, 0), jnp.sum(ti, 0)], 1)
    out_ref[...] = invert_right(both, lag_hi[...], lag_lo[...])


def local_kernel(
    own_ref, side_ref, core_ref, core_side_ref, q_ref, k_ref, v_ref, c_ref,
    fwd_hi, fwd_lo, inv_hi, inv_lo, taps_hi, taps_lo, mixed_ref, series_ref,
):
    x = (k_ref[...].astype(F32) * v_ref[...].astype(F32)).astype(BF16)
    g = (c_ref[...].astype(F32) * q_ref[...].astype(F32)).astype(BF16)
    xs = spectrum_left(fwd_hi[...], fwd_lo[...], x)
    gs = spectrum_left(fwd_hi[...], fwd_lo[...], g)
    count = own_ref.shape[0] // 8
    dp, far = lax.axis_index("dp"), lax.axis_index("ctx") // 16
    own, side = own_ref[...].astype(F32), side_ref[...].astype(F32)
    core, core_side = core_ref[0].astype(F32), core_side_ref[0].astype(F32)
    quarters = []
    for t in range(4):
        same = jnp.where(far == t % 2, own, side)
        cross = jnp.where(far == t % 2, core, core_side)
        quarters.append(jnp.where(dp == t // 2, same, cross).reshape(count, 8, SPAN))
    taps = jnp.concatenate(swap_blocks(quarters), 1).reshape(count * 32, SPAN).astype(BF16)
    nt = ((1,), (1,))
    hs = dot(taps_hi[...], taps, nt) + dot(taps_lo[...], taps, nt)
    zero = lax.broadcasted_iota(jnp.int32, (SPAN, x.shape[1]), 0) == 0
    hr, hi = hs[:SPAN], hs[SPAN:]
    mr, mi = multiply(xs[:SPAN], xs[SPAN:], hr, hi, zero, 1.0)
    mixed_ref[...] = invert_left(inv_hi[...], inv_lo[...], jnp.concatenate([mr, mi], 0))
    sr, si = multiply(gs[:SPAN], gs[SPAN:], hr, hi, zero, -1.0)
    series_ref[...] = invert_left(inv_hi[...], inv_lo[...], jnp.concatenate([sr, si], 0))


def taps_kernel(got_ref, pair_ref, after_ref, out_ref):
    del after_ref
    slots = got_ref.shape[0]
    core = lax.axis_index("dp")
    sums = []
    for far in range(2):
        place = 16 * (far ^ (TURN // 16))
        rows = got_ref[place:place + 16, 32:40, :].astype(F32)
        sums.append(jnp.sum(rows, axis=0))
    quarters = [jnp.where(core == t // 2, sums[t % 2], 0.0) for t in range(4)]
    near = jnp.concatenate(swap_blocks(quarters), 0)
    out_ref[:, :SPAN] = pair_ref[:, :SPAN] + near
    out_ref[:, SPAN:] = pair_ref[:, SPAN:]


def finish_kernel(
    table_ref, got_ref, mixed_ref, series_ref, k_ref, v_ref, c_ref,
    gq_ref, gk_ref, gv_ref, q_buf, k_buf, v_buf, sems,
):
    chunks = sems.shape[1]
    width = q_buf.shape[1] // chunks
    count = got_ref.shape[0] // chunks
    kind = table_ref[2, 0]
    copies = []
    for j in range(chunks):
        cols = slice(j * width, (j + 1) * width)
        place = (j ^ TURN_BLOCK) * count
        rows = got_ref[place:place + count, 0:32, :].reshape(width, SPAN)
        pair = jnp.transpose(rows).astype(F32)
        mixed = mixed_ref[:, cols] + jnp.where(kind == 2, pair, 0.0)
        series = series_ref[:, cols] + jnp.where(kind == 1, pair, 0.0)
        mixed = mixed.astype(BF16).astype(F32)
        series = series.astype(BF16).astype(F32)
        q_buf[:, cols] = (c_ref[:, cols].astype(F32) * mixed).astype(BF16)
        k_buf[:, cols] = (series * v_ref[:, cols].astype(F32)).astype(BF16)
        v_buf[:, cols] = (series * k_ref[:, cols].astype(F32)).astype(BF16)
        for i, (buf, ref) in enumerate(((q_buf, gq_ref), (k_buf, gk_ref), (v_buf, gv_ref))):
            copy = pltpu.make_async_copy(buf.at[:, cols], ref.at[:, cols], sems.at[i, j])
            copy.start()
            copies.append(copy)
    for copy in copies:
        copy.wait()


def taps_out_kernel(scale, own_ref, other_ref, out_ref):
    out_ref[...] = ((own_ref[...] + other_ref[...]) * scale).astype(BF16)


SMEM = pl.BlockSpec(memory_space=pltpu.SMEM)
VMEM = pl.BlockSpec(memory_space=pltpu.VMEM)
HBM = pl.BlockSpec(memory_space=pltpu.HBM)
ANY = pl.BlockSpec(memory_space=pl.ANY)
DMA = pltpu.SemaphoreType.DMA


def params(mebibytes=32):
    return pltpu.CompilerParams(vmem_limit_bytes=mebibytes * 1024 * 1024)


def cost(flops, moved):
    return pl.CostEstimate(flops=int(flops), bytes_accessed=int(moved), transcendentals=0)


def per_device(query, key, value, cotangent, filter_taps, span_slot, doc_lengths):
    parts = lax.axis_size("ctx")
    tokens, width = query.shape
    area = tokens * width
    pairs = parts - doc_lengths.shape[1]
    scale = float(tokens * parts * lax.axis_size("dp")) ** (-0.5)
    forward, inverse = transforms()

    def constant(matrix):
        return [jnp.asarray(m) for m in split_bf16(matrix)]

    fwd = constant(forward[:, :SPAN])
    fwd_t = constant(forward[:, :SPAN].T)
    inv = constant(inverse[:SPAN])
    inv_t = constant(inverse[:SPAN].T)
    tap_t = constant(np.roll(forward, -SPAN, 1).T)
    lag_t = constant(np.roll(inverse, SPAN, 0).T)
    core_swap = [(0, 1), (1, 0)]
    side_swap = [(c, c ^ 16) for c in range(parts)]
    block = 256
    steps = width // block
    group = block // 32
    wide = pl.BlockSpec((tokens, block), lambda i: (0, i))
    taps_rows = filter_taps.T

    def whole(array):
        return pl.BlockSpec(array.shape, lambda i: (0,) * array.ndim)

    def exchange(array):
        order = [[k ^ TURN for k in range(parts)]]
        return lax.all_to_all(
            array, "ctx", split_axis=0, concat_axis=0, axis_index_groups=order, tiled=True
        )

    chunk = jax.ShapeDtypeStruct((parts, 40, SPAN), BF16)
    out = pl.pallas_call(
        send_kernel,
        out_shape=chunk,
        in_specs=[HBM] * 7,
        out_specs=HBM,
        scratch_shapes=[
            pltpu.SMEM(span_slot.shape, jnp.int32),
            pltpu.SMEM(doc_lengths.shape, jnp.int32),
            pltpu.VMEM(taps_rows.shape, BF16),
        ] + [pltpu.VMEM((tokens, width), BF16)] * 4 + [
            pltpu.VMEM(chunk.shape, BF16), DMA((3,)), DMA((4, steps)), DMA((steps,)),
        ],
        compiler_params=params(60),
        cost_estimate=cost(2 * area, 8 * area),
        name="send",
    )(span_slot, doc_lengths, taps_rows, query, key, value, cotangent)
    got = exchange(out)

    two = pl.BlockSpec((2, group * 8, SPAN), lambda i: (0, i, 0))
    keep, give, table = pl.pallas_call(
        partial_kernel,
        grid=(steps,),
        out_shape=(
            jax.ShapeDtypeStruct((2, parts * 8, SPAN), F32),
            jax.ShapeDtypeStruct((2, parts * 8, SPAN), BF16),
            jax.ShapeDtypeStruct((3, pairs), jnp.int32),
        ),
        in_specs=[SMEM, SMEM] + [wide] * 4 + [whole(m) for m in fwd + inv],
        out_specs=(two, two, SMEM),
        scratch_shapes=[pltpu.SMEM((parts,), jnp.int32)],
        compiler_params=params(),
        cost_estimate=cost(2e9, 10 * area),
        name="partial_taps",
    )(span_slot, doc_lengths, query, key, value, cotangent, *fwd, *inv)
    taken = lax.ppermute(give, "dp", core_swap)

    keep, give = pl.pallas_call(
        halve_kernel,
        out_shape=(
            jax.ShapeDtypeStruct((parts * 8, SPAN), F32),
            jax.ShapeDtypeStruct((parts * 8, SPAN), BF16),
        ),
        in_specs=[VMEM, VMEM],
        out_specs=(VMEM, VMEM),
        compiler_params=params(),
        cost_estimate=cost(area, 3 * area),
        name="halve",
    )(keep, taken)
    near_other = lax.ppermute(give, "ctx", side_swap)

    back = pl.pallas_call(
        pair_kernel,
        out_shape=chunk,
        in_specs=[SMEM] + [VMEM] * 10,
        out_specs=VMEM,
        compiler_params=params(),
        cost_estimate=cost(1e9, 8 * area),
        name="pair",
    )(table, got, taps_rows, keep, near_other, *fwd_t, *inv_t, *tap_t)
    landed = exchange(back)

    own = got[:, 32:40, :].reshape(parts * 8, SPAN)
    side = lax.ppermute(own, "ctx", side_swap)
    core = lax.ppermute(jnp.stack([own, side]), "dp", core_swap)
    quarter = pl.BlockSpec((group * 8, SPAN), lambda i: (i ^ TURN_BLOCK, 0))
    mixed, series = pl.pallas_call(
        local_kernel,
        grid=(steps,),
        out_shape=(jax.ShapeDtypeStruct((tokens, width), F32),) * 2,
        in_specs=[
            quarter, quarter,
            pl.BlockSpec((1, group * 8, SPAN), lambda i: (0, i ^ TURN_BLOCK, 0)),
            pl.BlockSpec((1, group * 8, SPAN), lambda i: (1, i ^ TURN_BLOCK, 0)),
        ] + [wide] * 4 + [whole(m) for m in fwd + inv + fwd],
        out_specs=(wide, wide),
        compiler_params=params(),
        cost_estimate=cost(3e9, 20 * area),
        name="local",
    )(own, side, core, core, query, key, value, cotangent, *fwd, *inv, *fwd)

    pair_taps = pl.pallas_call(
        pair_taps_kernel,
        out_shape=jax.ShapeDtypeStruct((32, PTS), F32),
        in_specs=[SMEM] + [VMEM] * 5,
        out_specs=VMEM,
        compiler_params=params(),
        cost_estimate=cost(1e9, 6 * area),
        name="pair_taps",
    )(table, got, *fwd_t, *lag_t)
    taps_own = pl.pallas_call(
        taps_kernel,
        out_shape=jax.ShapeDtypeStruct((32, PTS), F32),
        in_specs=[VMEM, VMEM, ANY],
        out_specs=VMEM,
        compiler_params=params(),
        cost_estimate=cost(area, area),
        name="taps",
    )(landed, pair_taps, mixed)
    taps_other = lax.ppermute(taps_own, "dp", core_swap)

    result = jax.ShapeDtypeStruct((tokens, width), BF16)
    grads = pl.pallas_call(
        finish_kernel,
        out_shape=(result,) * 3,
        in_specs=[SMEM] + [VMEM] * 6,
        out_specs=(HBM,) * 3,
        scratch_shapes=[pltpu.VMEM((tokens, width), BF16)] * 3 + [DMA((3, steps))],
        compiler_params=params(),
        cost_estimate=cost(10 * area, 20 * area),
        name="finish",
    )(table, landed, mixed, series, key, value, cotangent)
    grad_filter = pl.pallas_call(
        functools.partial(taps_out_kernel, scale),
        out_shape=jax.ShapeDtypeStruct((32, PTS), BF16),
        in_specs=[VMEM] * 2,
        out_specs=VMEM,
        compiler_params=params(),
        name="taps_out",
    )(taps_own, taps_other)
    return (*grads, grad_filter.T)


def solution(mesh):
    return jax.shard_map(
        per_device,
        mesh=mesh,
        in_specs=(
            P(("dp", "ctx"), "ch"),
            P(("dp", "ctx"), "ch"),
            P(("dp", "ctx"), "ch"),
            P(("dp", "ctx"), "ch"),
            P(None, ("ch", "ctx")),
            P("dp", None),
            P("dp", None),
        ),
        out_specs=(
            P(("dp", "ctx"), "ch"),
            P(("dp", "ctx"), "ch"),
            P(("dp", "ctx"), "ch"),
            P(None, ("ch", "ctx")),
        ),
        check_vma=False,
    )
```

```python
import functools

import jax
import jax.numpy as jnp
import numpy as np
from jax import lax
from jax.experimental import pallas as pl
from jax.experimental.pallas import tpu as pltpu
from jax.sharding import PartitionSpec as P

SPAN = 128
PTS = 2 * SPAN
QUARTER = SPAN // 4
BLOCK = 256
TURN_OUT, TURN_BACK = 28, 24
F32, BF16 = jnp.float32, jnp.bfloat16


def split_bf16(matrix):
    high = matrix.astype(BF16)
    low = (matrix - high.astype(np.float64)).astype(BF16)
    return high, low


def transforms():
    freq = np.arange(SPAN)[:, None]
    point = np.arange(PTS)[None, :]
    angle = 2 * np.pi * ((freq * point) % PTS) / PTS
    real, imag = np.cos(angle), -np.sin(angle)
    imag[0] = np.where(np.arange(PTS) % 2 == 0, 1.0, -1.0)
    forward = np.concatenate([real, imag], 0)
    weight = np.full((PTS, 1), 2.0 / PTS)
    weight[0], weight[SPAN] = 1.0 / PTS, 1.0 / PTS
    inverse = (forward * weight).T
    return forward, inverse


def dot(a, b, dims=((1,), (0,))):
    return lax.dot_general(a, b, (dims, ((), ())), preferred_element_type=F32)


def halves(x):
    high = x.astype(BF16)
    return high, (x - high.astype(F32)).astype(BF16)


def spectrum_left(high, low, x):
    return dot(high, x) + dot(low, x)


def spectrum_right(x, high, low):
    return dot(x, high) + dot(x, low)


def invert_left(high, low, spec):
    s_high, s_low = halves(spec)
    return dot(high, s_high) + (dot(high, s_low) + dot(low, s_high))


def invert_right(spec, high, low):
    s_high, s_low = halves(spec)
    return dot(s_high, high) + (dot(s_low, high) + dot(s_high, low))


def multiply(ar, ai, br, bi, zero, sign):
    b_im = sign * jnp.where(zero, 0.0, bi)
    b_second = jnp.where(zero, bi, br)
    return ar * br - ai * b_im, ai * b_second + ar * b_im


def swap_blocks(parts):
    axis = parts[0].ndim - 1
    block = lax.broadcasted_iota(jnp.int32, parts[0].shape, axis) // QUARTER
    result = []
    for t in range(4):
        total = parts[t]
        for b in range(4):
            if b != t:
                moved = pltpu.roll(parts[b], (QUARTER * (b - t)) % SPAN, axis)
                total = jnp.where(block == b, moved, total)
        result.append(total)
    return result


def own_kind(slot_ref, len_ref):
    span = slot_ref[0, lax.axis_index("ctx")]

    def step(d, carry):
        pos, kind = carry
        length = len_ref[0, d]
        two = length == 2
        kind = jnp.where(two & (span == pos), 1, kind)
        kind = jnp.where(two & (span == pos + 1), 2, kind)
        return pos + length, kind

    zero = jnp.int32(0)
    return lax.fori_loop(0, len_ref.shape[1], step, (zero, zero))[1]


def send_kernel(
    slot_hbm, len_hbm, taps_hbm, q_hbm, k_hbm, v_hbm, c_hbm, out_hbm,
    slot_ref, len_ref, taps_ref, q_buf, k_buf, v_buf, c_buf, out_buf,
    small_sem, in_sem, out_sem,
):
    chunks = out_sem.shape[0]
    width = q_buf.shape[1] // chunks
    count = out_buf.shape[0] // chunks
    small = [
        pltpu.make_async_copy(src, dst, small_sem.at[i])
        for i, (src, dst) in enumerate(
            ((slot_hbm, slot_ref), (len_hbm, len_ref), (taps_hbm, taps_ref))
        )
    ]
    small[0].start()
    small[1].start()
    wide = []
    for j in range(chunks):
        cols = pl.ds(j * width, width)
        wide.append([
            pltpu.make_async_copy(src.at[:, cols], dst.at[:, cols], in_sem.at[i, j])
            for i, (src, dst) in enumerate(
                ((k_hbm, k_buf), (v_hbm, v_buf), (c_hbm, c_buf), (q_hbm, q_buf))
            )
        ])
        for copy in wide[-1]:
            copy.start()
        if j == 0:
            small[2].start()
    small[0].wait()
    small[1].wait()
    first = own_kind(slot_ref, len_ref) == 1
    small[2].wait()
    taps = taps_ref[:, 0:SPAN].astype(F32)
    quarters = swap_blocks([taps[8 * b:8 * b + 8] for b in range(4)])
    core = lax.axis_index("dp") == 0
    outs = []
    for j in range(chunks):
        for copy in wide[j]:
            copy.wait()
        cols = slice(j * width, (j + 1) * width)
        a = jnp.where(first, k_buf[:, cols].astype(F32), c_buf[:, cols].astype(F32))
        b = jnp.where(first, v_buf[:, cols].astype(F32), q_buf[:, cols].astype(F32))
        series = jnp.transpose((a * b).astype(BF16)).reshape(count, 32, SPAN)
        far = int(2 * j >= chunks)
        mine = jnp.where(core, quarters[far], quarters[2 + far]).astype(BF16)
        for piece in range(0, count, 4):
            rows = pl.ds((j * count + piece) ^ TURN_OUT, 4)
            out_buf[rows, 0:32, :] = series[piece:piece + 4]
            out_buf[rows, 32:40, :] = jnp.broadcast_to(mine[None], (4, 8, SPAN))
        rows = pl.ds((j * count) ^ (TURN_OUT // count * count), count)
        out = pltpu.make_async_copy(out_buf.at[rows], out_hbm.at[rows], out_sem.at[j])
        out.start()
        outs.append(out)
    for out in outs:
        out.wait()


def partial_kernel(
    q_ref, k_ref, v_ref, c_ref, fwd_hi, fwd_lo, inv_hi, inv_lo, give_ref
):
    blocks = q_ref.shape[1] // BLOCK
    count = BLOCK // 32
    zero = lax.broadcasted_iota(jnp.int32, (SPAN, BLOCK), 0) == 0
    for j in range(blocks):
        cols = slice(j * BLOCK, (j + 1) * BLOCK)
        x = (k_ref[:, cols].astype(F32) * v_ref[:, cols].astype(F32)).astype(BF16)
        g = (c_ref[:, cols].astype(F32) * q_ref[:, cols].astype(F32)).astype(BF16)
        xs = spectrum_left(fwd_hi[...], fwd_lo[...], x)
        gs = spectrum_left(fwd_hi[...], fwd_lo[...], g)
        pr, pi = multiply(gs[:SPAN], gs[SPAN:], xs[:SPAN], xs[SPAN:], zero, -1.0)
        taps = invert_left(inv_hi[...], inv_lo[...], jnp.concatenate([pr, pi], 0))
        rows = jnp.transpose(taps).reshape(count, 4, 8, SPAN)
        quarters = swap_blocks([rows[:, b] for b in range(4)])
        for t in range(4):
            packed = quarters[t].reshape(count * 8, SPAN).astype(BF16)
            give_ref[t, j * count * 8:(j + 1) * count * 8, :] = packed


def tables_kernel(
    slot_ref, len_ref, taps_ref, tap_hi, tap_lo, after_ref, table_ref, spec_ref, inverse_ref
):
    del after_ref
    spec_ref[...] = spectrum_right(taps_ref[...], tap_hi[...], tap_lo[...])

    def fill(r, carry):
        inverse_ref[slot_ref[0, r]] = r
        return carry

    lax.fori_loop(0, slot_ref.shape[1], fill, 0)

    def step(d, carry):
        pos, count = carry
        length = len_ref[0, d]

        @pl.when(length == 2)
        def _():
            table_ref[0, count] = inverse_ref[pos]
            table_ref[1, count] = inverse_ref[pos + 1]

        return pos + length, count + length - 1

    lax.fori_loop(0, len_ref.shape[1], step, (jnp.int32(0), jnp.int32(0)))
    table_ref[2, 0] = own_kind(slot_ref, len_ref)


def share_kernel(own_ref, other_ref, keep_ref, side_ref, next_ref, cross_ref):
    ctx = lax.axis_index("ctx")
    far, odd = ctx // 16, ctx % 2

    def total(t):
        return own_ref[t].astype(F32) + other_ref[t].astype(F32)

    keep_ref[...] = total(2 * far + odd)
    side_ref[...] = total(2 * (1 - far) + odd).astype(BF16)
    next_ref[...] = total(2 * far + 1 - odd).astype(BF16)
    cross_ref[...] = total(2 * (1 - far) + 1 - odd).astype(BF16)


def pair_spectra(table_ref, got_ref, fwd_hi, fwd_lo):
    pairs = table_ref.shape[1]
    rows = [got_ref[table_ref[k, p] ^ TURN_OUT, 0:32, :] for k in range(2) for p in range(pairs)]
    spec = spectrum_right(jnp.concatenate(rows, 0), fwd_hi[...], fwd_lo[...])
    return spec.reshape(2, pairs, 32, PTS)


def pair_kernel(
    table_ref, got_ref, spec_ref, keep_ref, side_ref, next_ref, cross_ref,
    fwd_hi, fwd_lo, inv_hi, inv_lo, out_ref,
):
    slots, pairs = got_ref.shape[0], table_ref.shape[1]
    hr, hi = spec_ref[:, :SPAN], spec_ref[:, SPAN:]
    zero = lax.broadcasted_iota(jnp.int32, hr.shape, 1) == 0
    spec = pair_spectra(table_ref, got_ref, fwd_hi, fwd_lo)
    out_ref[:, 0:32, :] = jnp.zeros((slots, 32, SPAN), BF16)
    for k in range(2):
        sr, si = spec[k, :, :, :SPAN], spec[k, :, :, SPAN:]
        pr, pi = multiply(sr, si, hr[None], hi[None], zero[None], 1.0 if k == 0 else -1.0)
        both = jnp.concatenate([pr, pi], 2).reshape(pairs * 32, PTS)
        result = invert_right(both, inv_hi[...], inv_lo[...]).astype(BF16)
        for p in range(pairs):
            out_ref[table_ref[1 - k, p] ^ TURN_BACK, 0:32, :] = result[32 * p:32 * p + 32]
    near = keep_ref[...] + side_ref[...].astype(F32)
    near = (near + (next_ref[...].astype(F32) + cross_ref[...].astype(F32))).astype(BF16)
    near = near.reshape(slots, 8, SPAN)
    for j in range(slots // 8):
        place = 8 * (j ^ (TURN_BACK // 8))
        out_ref[place:place + 8, 32:40, :] = near[8 * j:8 * j + 8]


def pair_taps_kernel(table_ref, got_ref, fwd_hi, fwd_lo, lag_hi, lag_lo, out_ref):
    spec = pair_spectra(table_ref, got_ref, fwd_hi, fwd_lo)
    zero = lax.broadcasted_iota(jnp.int32, (1, 32, SPAN), 2) == 0
    xs, gs = spec[0], spec[1]
    tr, ti = multiply(
        gs[:, :, :SPAN], gs[:, :, SPAN:], xs[:, :, :SPAN], xs[:, :, SPAN:], zero, -1.0
    )
    both = jnp.concatenate([jnp.sum(tr, 0), jnp.sum(ti, 0)], 1)
    taps = invert_right(both, lag_hi[...], lag_lo[...]).astype(BF16)
    out_ref[0:32, :] = taps[:, :SPAN]
    out_ref[32:64, :] = taps[:, SPAN:]


def local_kernel(
    own_ref, core_ref, q_ref, k_ref, v_ref, c_ref, fwd_hi, fwd_lo, inv_hi, inv_lo,
    mixed_ref, series_ref,
):
    blocks = q_ref.shape[1] // BLOCK
    count = BLOCK // 32
    dp, far = lax.axis_index("dp"), lax.axis_index("ctx") // 16
    zero = lax.broadcasted_iota(jnp.int32, (SPAN, BLOCK), 0) == 0
    nt = ((1,), (1,))
    for j in range(blocks):
        cols = slice(j * BLOCK, (j + 1) * BLOCK)
        x = (k_ref[:, cols].astype(F32) * v_ref[:, cols].astype(F32)).astype(BF16)
        g = (c_ref[:, cols].astype(F32) * q_ref[:, cols].astype(F32)).astype(BF16)
        xs = spectrum_left(fwd_hi[...], fwd_lo[...], x)
        gs = spectrum_left(fwd_hi[...], fwd_lo[...], g)

        def rows(ref, start):
            places = [start + 32 * (b ^ (TURN_OUT // 4)) for b in (2 * j, 2 * j + 1)]
            return jnp.concatenate([ref[p:p + 32, :].astype(F32) for p in places], 0)

        own, side = rows(own_ref, 0), rows(own_ref, 256)
        core, cross = rows(core_ref, 0), rows(core_ref, 256)
        quarters = []
        for t in range(4):
            here = jnp.where(far == t % 2, own, side)
            there = jnp.where(far == t % 2, core, cross)
            quarters.append(jnp.where(dp == t // 2, here, there).reshape(count, 8, SPAN))
        taps = jnp.concatenate(swap_blocks(quarters), 1).reshape(BLOCK, SPAN).astype(BF16)
        hs = dot(fwd_hi[...], taps, nt) + dot(fwd_lo[...], taps, nt)
        hr, hi = hs[:SPAN], hs[SPAN:]
        mr, mi = multiply(xs[:SPAN], xs[SPAN:], hr, hi, zero, 1.0)
        spec = jnp.concatenate([mr, mi], 0)
        mixed_ref[:, cols] = invert_left(inv_hi[...], inv_lo[...], spec)
        sr, si = multiply(gs[:SPAN], gs[SPAN:], hr, hi, zero, -1.0)
        spec = jnp.concatenate([sr, si], 0)
        series_ref[:, cols] = invert_left(inv_hi[...], inv_lo[...], spec)


def finish_kernel(
    scale, table_ref, got_ref, mixed_ref, series_ref, k_ref, v_ref, c_ref, own_ref, core_ref,
    gq_ref, gk_ref, gv_ref, gf_ref, q_buf, k_buf, v_buf, f_buf, sems, f_sem,
):
    chunks = sems.shape[1]
    width = q_buf.shape[1] // chunks
    slots = got_ref.shape[0]
    count = slots // chunks
    kind = table_ref[2, 0]
    copies = []

    def filter_taps():
        quarters = []
        for t in range(4):
            sources = [s ^ TURN_BACK for s in range(slots) if 2 * (s // 16) + s % 2 == t]
            quarters.append(sum(got_ref[s, 32:40, :].astype(F32) for s in sources))
        near = jnp.concatenate(swap_blocks(quarters), 0)
        pair = own_ref[512:576, :].astype(F32) + core_ref[512:576, :].astype(F32)
        f_buf[:, :SPAN] = ((near + pair[:32]) * scale).astype(BF16)
        f_buf[:, SPAN:] = (pair[32:] * scale).astype(BF16)
        copy = pltpu.make_async_copy(f_buf, gf_ref, f_sem.at[0])
        copy.start()
        copies.append(copy)

    for j in range(chunks):
        cols = slice(j * width, (j + 1) * width)
        place = (j ^ (TURN_BACK // count)) * count
        rows = got_ref[place:place + count, 0:32, :].reshape(width, SPAN)
        pair = jnp.transpose(rows).astype(F32)
        mixed = mixed_ref[:, cols] + jnp.where(kind == 2, pair, 0.0)
        series = series_ref[:, cols] + jnp.where(kind == 1, pair, 0.0)
        mixed = mixed.astype(BF16).astype(F32)
        series = series.astype(BF16).astype(F32)
        q_buf[:, cols] = (c_ref[:, cols].astype(F32) * mixed).astype(BF16)
        k_buf[:, cols] = (series * v_ref[:, cols].astype(F32)).astype(BF16)
        v_buf[:, cols] = (series * k_ref[:, cols].astype(F32)).astype(BF16)
        for i, (buf, ref) in enumerate(((q_buf, gq_ref), (k_buf, gk_ref), (v_buf, gv_ref))):
            copy = pltpu.make_async_copy(buf.at[:, cols], ref.at[:, cols], sems.at[i, j])
            copy.start()
            copies.append(copy)
        if j == 1:
            filter_taps()
    for copy in copies:
        copy.wait()


SMEM = pl.BlockSpec(memory_space=pltpu.SMEM)
VMEM = pl.BlockSpec(memory_space=pltpu.VMEM)
HBM = pl.BlockSpec(memory_space=pltpu.HBM)
ANY = pl.BlockSpec(memory_space=pl.ANY)
DMA = pltpu.SemaphoreType.DMA


def params(mebibytes=32):
    return pltpu.CompilerParams(vmem_limit_bytes=mebibytes * 1024 * 1024)


def cost(flops, moved):
    return pl.CostEstimate(flops=int(flops), bytes_accessed=int(moved), transcendentals=0)


def per_device(query, key, value, cotangent, filter_taps, span_slot, doc_lengths):
    parts = lax.axis_size("ctx")
    tokens, width = query.shape
    area = tokens * width
    pairs = parts - doc_lengths.shape[1]
    scale = float(tokens * parts * lax.axis_size("dp")) ** (-0.5)
    forward, inverse = transforms()

    def constant(matrix):
        return [jnp.asarray(m) for m in split_bf16(matrix)]

    fwd = constant(forward[:, :SPAN])
    fwd_t = constant(forward[:, :SPAN].T)
    inv = constant(inverse[:SPAN])
    inv_t = constant(inverse[:SPAN].T)
    tap_t = constant(np.roll(forward, -SPAN, 1).T)
    lag_t = constant(np.roll(inverse, SPAN, 0).T)
    core_swap = [(0, 1), (1, 0)]
    side_swap = [(c, c ^ 16) for c in range(parts)]
    cross_swap = [(c, c ^ 17) for c in range(parts)]
    next_swap = [(c, c ^ 1) for c in range(parts)]
    steps = width // BLOCK
    taps_rows = filter_taps.T

    def exchange(array, turn):
        order = [[k ^ turn for k in range(parts)]]
        return lax.all_to_all(
            array, "ctx", split_axis=0, concat_axis=0, axis_index_groups=order, tiled=True
        )

    chunk = jax.ShapeDtypeStruct((parts, 40, SPAN), BF16)
    out = pl.pallas_call(
        send_kernel,
        out_shape=chunk,
        in_specs=[HBM] * 7,
        out_specs=HBM,
        scratch_shapes=[
            pltpu.SMEM(span_slot.shape, jnp.int32),
            pltpu.SMEM(doc_lengths.shape, jnp.int32),
            pltpu.VMEM(taps_rows.shape, BF16),
        ] + [pltpu.VMEM((tokens, width), BF16)] * 4 + [
            pltpu.VMEM(chunk.shape, BF16), DMA((3,)), DMA((4, 2)), DMA((2,)),
        ],
        compiler_params=params(60),
        cost_estimate=cost(2 * area, 8 * area),
        name="send",
    )(span_slot, doc_lengths, taps_rows, query, key, value, cotangent)
    got = exchange(out, TURN_OUT)

    give = pl.pallas_call(
        partial_kernel,
        out_shape=jax.ShapeDtypeStruct((4, parts * 8, SPAN), BF16),
        in_specs=[VMEM] * 8,
        out_specs=VMEM,
        compiler_params=params(),
        cost_estimate=cost(2e9, 10 * area),
        name="partial_taps",
    )(query, key, value, cotangent, *fwd, *inv)
    taken = lax.ppermute(give, "dp", core_swap)
    quarter = jax.ShapeDtypeStruct((parts * 8, SPAN), BF16)
    keep, side, near, cross = pl.pallas_call(
        share_kernel,
        out_shape=(jax.ShapeDtypeStruct(quarter.shape, F32), quarter, quarter, quarter),
        in_specs=[VMEM, VMEM],
        out_specs=(VMEM,) * 4,
        compiler_params=params(),
        cost_estimate=cost(area, 3 * area),
        name="share",
    )(give, taken)
    table, tap_spec = pl.pallas_call(
        tables_kernel,
        out_shape=(
            jax.ShapeDtypeStruct((3, pairs), jnp.int32),
            jax.ShapeDtypeStruct((32, PTS), F32),
        ),
        in_specs=[SMEM, SMEM, VMEM, VMEM, VMEM, ANY],
        out_specs=(SMEM, VMEM),
        scratch_shapes=[pltpu.SMEM((parts,), jnp.int32)],
        compiler_params=params(),
        cost_estimate=cost(area, area),
        name="tables",
    )(span_slot, doc_lengths, taps_rows, *tap_t, cross)
    side = lax.ppermute(side, "ctx", side_swap)
    near = lax.ppermute(near, "ctx", next_swap)
    cross = lax.ppermute(cross, "ctx", cross_swap)

    back = pl.pallas_call(
        pair_kernel,
        out_shape=chunk,
        in_specs=[SMEM] + [VMEM] * 10,
        out_specs=VMEM,
        compiler_params=params(),
        cost_estimate=cost(1e9, 8 * area),
        name="pair",
    )(table, got, tap_spec, keep, side, near, cross, *fwd_t, *inv_t)
    landed = exchange(back, TURN_BACK)

    own = got[:, 32:40, :].reshape(parts * 8, SPAN)
    pair_taps = pl.pallas_call(
        pair_taps_kernel,
        out_shape=jax.ShapeDtypeStruct((64, SPAN), BF16),
        in_specs=[SMEM] + [VMEM] * 5,
        out_specs=VMEM,
        compiler_params=params(),
        cost_estimate=cost(1e9, 6 * area),
        name="pair_taps",
    )(table, got, *fwd_t, *lag_t)
    own = jnp.concatenate([own, lax.ppermute(own, "ctx", side_swap), pair_taps], 0)
    core = lax.ppermute(own, "dp", core_swap)
    mixed, series = pl.pallas_call(
        local_kernel,
        out_shape=(jax.ShapeDtypeStruct((tokens, width), F32),) * 2,
        in_specs=[VMEM] * 10,
        out_specs=(VMEM, VMEM),
        compiler_params=params(),
        cost_estimate=cost(3e9, 20 * area),
        name="local",
    )(own, core, query, key, value, cotangent, *fwd, *inv)

    result = jax.ShapeDtypeStruct((tokens, width), BF16)
    *grads, grad_filter = pl.pallas_call(
        functools.partial(finish_kernel, scale),
        out_shape=(result,) * 3 + (jax.ShapeDtypeStruct((32, PTS), BF16),),
        in_specs=[SMEM] + [VMEM] * 8,
        out_specs=(HBM,) * 4,
        scratch_shapes=[pltpu.VMEM((tokens, width), BF16)] * 3
        + [pltpu.VMEM((32, PTS), BF16), DMA((3, steps)), DMA((1,))],
        compiler_params=params(),
        cost_estimate=cost(10 * area, 20 * area),
        name="finish",
    )(table, landed, mixed, series, key, value, cotangent, own, core)
    return (*grads, grad_filter.T)


def solution(mesh):
    return jax.shard_map(
        per_device,
        mesh=mesh,
        in_specs=(
            P(("dp", "ctx"), "ch"),
            P(("dp", "ctx"), "ch"),
            P(("dp", "ctx"), "ch"),
            P(("dp", "ctx"), "ch"),
            P(None, ("ch", "ctx")),
            P("dp", None),
            P("dp", None),
        ),
        out_specs=(
            P(("dp", "ctx"), "ch"),
            P(("dp", "ctx"), "ch"),
            P(("dp", "ctx"), "ch"),
            P(None, ("ch", "ctx")),
        ),
        check_vma=False,
    )
```

```python
import functools

import jax
import jax.numpy as jnp
import numpy as np
from jax import lax
from jax.experimental import pallas as pl
from jax.experimental.pallas import tpu as pltpu
from jax.sharding import PartitionSpec as P

SPAN = 128
PTS = 2 * SPAN
QUARTER = SPAN // 4
BLOCK = 1024
TURN_OUT, TURN_BACK = 28, 24
F32, BF16 = jnp.float32, jnp.bfloat16


def split_bf16(matrix):
    high = matrix.astype(BF16)
    low = (matrix - high.astype(np.float64)).astype(BF16)
    return high, low


def transforms():
    freq = np.arange(SPAN)[:, None]
    point = np.arange(PTS)[None, :]
    angle = 2 * np.pi * ((freq * point) % PTS) / PTS
    real, imag = np.cos(angle), -np.sin(angle)
    imag[0] = np.where(np.arange(PTS) % 2 == 0, 1.0, -1.0)
    forward = np.concatenate([real, imag], 0)
    weight = np.full((PTS, 1), 2.0 / PTS)
    weight[0], weight[SPAN] = 1.0 / PTS, 1.0 / PTS
    inverse = (forward * weight).T
    return forward, inverse


def dot(a, b, dims=((1,), (0,))):
    return lax.dot_general(a, b, (dims, ((), ())), preferred_element_type=F32)


def halves(x):
    high = x.astype(BF16)
    return high, (x - high.astype(F32)).astype(BF16)


def spectrum_left(both, x):
    return dot(both, jnp.concatenate([x, x], 0))


def spectrum_right(x, both):
    return dot(jnp.concatenate([x, x], 1), both)


def invert_left(both, spec):
    s_high, s_low = halves(spec)
    main = dot(both, s_high)
    return main[:SPAN] + (main[SPAN:] + dot(both[:SPAN], s_low))


def invert_right(spec, both):
    s_high, s_low = halves(spec)
    main = dot(s_high, both)
    count = both.shape[1] // 2
    return main[:, :count] + (main[:, count:] + dot(s_low, both[:, :count]))


def multiply(ar, ai, br, bi, zero, sign):
    b_im = sign * jnp.where(zero, 0.0, bi)
    b_second = jnp.where(zero, bi, br)
    return ar * br - ai * b_im, ai * b_second + ar * b_im


def swap_blocks(parts):
    axis = parts[0].ndim - 1
    block = lax.broadcasted_iota(jnp.int32, parts[0].shape, axis) // QUARTER
    result = []
    for t in range(4):
        total = parts[t]
        for b in range(4):
            if b != t:
                moved = pltpu.roll(parts[b], (QUARTER * (b - t)) % SPAN, axis)
                total = jnp.where(block == b, moved, total)
        result.append(total)
    return result


def own_kind(slot_ref, len_ref):
    span = slot_ref[0, lax.axis_index("ctx")]

    def step(d, carry):
        pos, kind = carry
        length = len_ref[0, d]
        two = length == 2
        kind = jnp.where(two & (span == pos), 1, kind)
        kind = jnp.where(two & (span == pos + 1), 2, kind)
        return pos + length, kind

    zero = jnp.int32(0)
    return lax.fori_loop(0, len_ref.shape[1], step, (zero, zero), unroll=True)[1]


def send_kernel(
    slot_hbm, len_hbm, taps_hbm, q_hbm, k_hbm, v_hbm, c_hbm, out_hbm,
    slot_ref, len_ref, taps_ref, q_buf, k_buf, v_buf, c_buf, out_buf,
    small_sem, in_sem, out_sem,
):
    chunks = out_sem.shape[0]
    width = q_buf.shape[1] // chunks
    count = out_buf.shape[0] // chunks
    small = [
        pltpu.make_async_copy(src, dst, small_sem.at[i])
        for i, (src, dst) in enumerate(
            ((slot_hbm, slot_ref), (len_hbm, len_ref), (taps_hbm, taps_ref))
        )
    ]
    small[0].start()
    small[1].start()
    wide = []
    for j in range(chunks):
        cols = pl.ds(j * width, width)
        wide.append([
            pltpu.make_async_copy(src.at[:, cols], dst.at[:, cols], in_sem.at[i, j])
            for i, (src, dst) in enumerate(
                ((k_hbm, k_buf), (v_hbm, v_buf), (c_hbm, c_buf), (q_hbm, q_buf))
            )
        ])
        for copy in wide[-1]:
            copy.start()
        if j == 0:
            small[2].start()
    small[0].wait()
    small[1].wait()
    first = own_kind(slot_ref, len_ref) == 1
    small[2].wait()
    taps = taps_ref[:, 0:SPAN].astype(F32)
    quarters = swap_blocks([taps[8 * b:8 * b + 8] for b in range(4)])
    core = lax.axis_index("dp") == 0
    outs = []
    for j in range(chunks):
        for copy in wide[j]:
            copy.wait()
        cols = slice(j * width, (j + 1) * width)
        a = jnp.where(first, k_buf[:, cols].astype(F32), c_buf[:, cols].astype(F32))
        b = jnp.where(first, v_buf[:, cols].astype(F32), q_buf[:, cols].astype(F32))
        series = jnp.transpose((a * b).astype(BF16)).reshape(count, 32, SPAN)
        far = int(2 * j >= chunks)
        mine = jnp.where(core, quarters[far], quarters[2 + far]).astype(BF16)
        for piece in range(0, count, 4):
            rows = pl.ds((j * count + piece) ^ TURN_OUT, 4)
            out_buf[rows, 0:32, :] = series[piece:piece + 4]
            out_buf[rows, 32:40, :] = jnp.broadcast_to(mine[None], (4, 8, SPAN))
        rows = pl.ds((j * count) ^ (TURN_OUT // count * count), count)
        out = pltpu.make_async_copy(out_buf.at[rows], out_hbm.at[rows], out_sem.at[j])
        out.start()
        outs.append(out)
    for out in outs:
        out.wait()


def partial_kernel(
    q_ref, k_ref, v_ref, c_ref, fwd, inv, give_ref
):
    blocks = q_ref.shape[1] // BLOCK
    count = BLOCK // 32
    zero = lax.broadcasted_iota(jnp.int32, (SPAN, BLOCK), 0) == 0
    for j in range(blocks):
        cols = slice(j * BLOCK, (j + 1) * BLOCK)
        x = (k_ref[:, cols].astype(F32) * v_ref[:, cols].astype(F32)).astype(BF16)
        g = (c_ref[:, cols].astype(F32) * q_ref[:, cols].astype(F32)).astype(BF16)
        xs = spectrum_left(fwd[...], x)
        gs = spectrum_left(fwd[...], g)
        pr, pi = multiply(gs[:SPAN], gs[SPAN:], xs[:SPAN], xs[SPAN:], zero, -1.0)
        taps = invert_left(inv[...], jnp.concatenate([pr, pi], 0))
        rows = jnp.transpose(taps).reshape(count, 4, 8, SPAN)
        quarters = swap_blocks([rows[:, b] for b in range(4)])
        for t in range(4):
            packed = quarters[t].reshape(count * 8, SPAN).astype(BF16)
            give_ref[t, j * count * 8:(j + 1) * count * 8, :] = packed


def tables_kernel(
    slot_ref, len_ref, taps_ref, tap, after_ref, table_ref, spec_ref, inverse_ref
):
    del after_ref
    spec_ref[...] = spectrum_right(taps_ref[...], tap[...])

    slots = slot_ref.shape[1]

    def fill(r, carry):
        inverse_ref[slot_ref[0, r]] = r
        return carry

    lax.fori_loop(0, slots, fill, 0, unroll=True)

    def step(d, carry):
        pos, count = carry
        length = len_ref[0, d]
        table_ref[0, count] = inverse_ref[pos]
        table_ref[1, count] = inverse_ref[jnp.minimum(pos + 1, slots - 1)]
        return pos + length, count + length - 1

    zero = jnp.int32(0)
    lax.fori_loop(0, len_ref.shape[1], step, (zero, zero), unroll=True)
    table_ref[2, 0] = own_kind(slot_ref, len_ref)


def share_kernel(own_ref, other_ref, keep_ref, side_ref, next_ref, cross_ref):
    ctx = lax.axis_index("ctx")
    far, odd = ctx // 16, ctx % 2

    def total(t):
        return own_ref[t].astype(F32) + other_ref[t].astype(F32)

    keep_ref[...] = total(2 * far + odd)
    side_ref[...] = total(2 * (1 - far) + odd).astype(BF16)
    next_ref[...] = total(2 * far + 1 - odd).astype(BF16)
    cross_ref[...] = total(2 * (1 - far) + 1 - odd).astype(BF16)


def pair_spectra(table_ref, got_ref, fwd):
    pairs = table_ref.shape[1] // 2
    rows = [got_ref[table_ref[k, p] ^ TURN_OUT, 0:32, :] for k in range(2) for p in range(pairs)]
    spec = spectrum_right(jnp.concatenate(rows, 0), fwd[...])
    return spec.reshape(2, pairs, 32, PTS)


def pair_kernel(
    table_ref, got_ref, spec_ref, fwd, inv, out_ref
):
    slots, pairs = got_ref.shape[0], table_ref.shape[1] // 2
    hr, hi = spec_ref[:, :SPAN], spec_ref[:, SPAN:]
    zero = lax.broadcasted_iota(jnp.int32, hr.shape, 1) == 0
    spec = pair_spectra(table_ref, got_ref, fwd)
    out_ref[...] = jnp.zeros((slots, 32, SPAN), BF16)
    for k in range(2):
        sr, si = spec[k, :, :, :SPAN], spec[k, :, :, SPAN:]
        pr, pi = multiply(sr, si, hr[None], hi[None], zero[None], 1.0 if k == 0 else -1.0)
        both = jnp.concatenate([pr, pi], 2).reshape(pairs * 32, PTS)
        result = invert_right(both, inv[...]).astype(BF16)
        for p in range(pairs):
            out_ref[table_ref[1 - k, p] ^ TURN_BACK] = result[32 * p:32 * p + 32]


def load_kernel(
    pair_ref, keep_ref, side_ref, next_ref, cross_ref, out_hbm, out_buf, sems
):
    slots = pair_ref.shape[0]
    half = slots // 2
    copies = []
    for h in range(2):
        source = slice(h * half * 8, (h + 1) * half * 8)
        near = keep_ref[source] + side_ref[source].astype(F32)
        near = near + (next_ref[source].astype(F32) + cross_ref[source].astype(F32))
        near = near.astype(BF16).reshape(half, 8, SPAN)
        start = (h * half) ^ (TURN_BACK // half * half)
        rows = slice(start, start + half)
        out_buf[rows, 0:32, :] = pair_ref[rows]
        for piece in range(0, half, 8):
            place = (h * half + piece) ^ TURN_BACK
            out_buf[place:place + 8, 32:40, :] = near[piece:piece + 8]
        copy = pltpu.make_async_copy(out_buf.at[rows], out_hbm.at[rows], sems.at[h])
        copy.start()
        copies.append(copy)
    for copy in copies:
        copy.wait()


def pair_taps_kernel(
    table_ref, got_ref, q_ref, k_ref, v_ref, c_ref, fwd, own_fwd, lag,
    out_ref, xs_ref, gs_ref,
):
    for j in range(q_ref.shape[1] // BLOCK):
        cols = slice(j * BLOCK, (j + 1) * BLOCK)
        x = (k_ref[:, cols].astype(F32) * v_ref[:, cols].astype(F32)).astype(BF16)
        g = (c_ref[:, cols].astype(F32) * q_ref[:, cols].astype(F32)).astype(BF16)
        xs_ref[:, cols] = spectrum_left(own_fwd[...], x)
        gs_ref[:, cols] = spectrum_left(own_fwd[...], g)
    spec = pair_spectra(table_ref, got_ref, fwd)
    zero = lax.broadcasted_iota(jnp.int32, (1, 32, SPAN), 2) == 0
    xs, gs = spec[0], spec[1]
    tr, ti = multiply(
        gs[:, :, :SPAN], gs[:, :, SPAN:], xs[:, :, :SPAN], xs[:, :, SPAN:], zero, -1.0
    )
    both = jnp.concatenate([jnp.sum(tr, 0), jnp.sum(ti, 0)], 1)
    taps = invert_right(both, lag[...]).astype(BF16)
    out_ref[0:32, :] = taps[:, :SPAN]
    out_ref[32:64, :] = taps[:, SPAN:]


def local_kernel(
    own_ref, core_ref, xs_ref, gs_ref, fwd, inv, mixed_ref, series_ref
):
    blocks = xs_ref.shape[1] // BLOCK
    count = BLOCK // 32
    dp, far = lax.axis_index("dp"), lax.axis_index("ctx") // 16
    zero = lax.broadcasted_iota(jnp.int32, (SPAN, BLOCK), 0) == 0
    nt = ((1,), (1,))
    for j in range(blocks):
        cols = slice(j * BLOCK, (j + 1) * BLOCK)
        xs, gs = xs_ref[:, cols], gs_ref[:, cols]

        def rows(ref, start):
            blocks = range(j * BLOCK // SPAN, (j + 1) * BLOCK // SPAN)
            places = [start + 32 * (b ^ (TURN_OUT // 4)) for b in blocks]
            return jnp.concatenate([ref[p:p + 32, :].astype(F32) for p in places], 0)

        own, side = rows(own_ref, 0), rows(own_ref, 256)
        core, cross = rows(core_ref, 0), rows(core_ref, 256)
        quarters = []
        for t in range(4):
            here = jnp.where(far == t % 2, own, side)
            there = jnp.where(far == t % 2, core, cross)
            quarters.append(jnp.where(dp == t // 2, here, there).reshape(count, 8, SPAN))
        taps = jnp.concatenate(swap_blocks(quarters), 1).reshape(BLOCK, SPAN).astype(BF16)
        hs = dot(fwd[...], jnp.concatenate([taps, taps], 1), nt)
        hr, hi = hs[:SPAN], hs[SPAN:]
        mr, mi = multiply(xs[:SPAN], xs[SPAN:], hr, hi, zero, 1.0)
        spec = jnp.concatenate([mr, mi], 0)
        mixed_ref[:, cols] = invert_left(inv[...], spec)
        sr, si = multiply(gs[:SPAN], gs[SPAN:], hr, hi, zero, -1.0)
        spec = jnp.concatenate([sr, si], 0)
        series_ref[:, cols] = invert_left(inv[...], spec)


def finish_kernel(
    scale, table_ref, got_ref, mixed_ref, series_ref, k_ref, v_ref, c_ref, own_ref, core_ref,
    gq_ref, gk_ref, gv_ref, gf_ref, q_buf, k_buf, v_buf, f_buf, sems, f_sem,
):
    chunks = sems.shape[1]
    width = q_buf.shape[1] // chunks
    slots = got_ref.shape[0]
    count = slots // chunks
    kind = table_ref[2, 0]
    copies = []

    def filter_taps():
        quarters = []
        for t in range(4):
            sources = [s ^ TURN_BACK for s in range(slots) if 2 * (s // 16) + s % 2 == t]
            quarters.append(sum(got_ref[s, 32:40, :].astype(F32) for s in sources))
        near = jnp.concatenate(swap_blocks(quarters), 0)
        pair = own_ref[512:576, :].astype(F32) + core_ref[512:576, :].astype(F32)
        f_buf[:, :SPAN] = ((near + pair[:32]) * scale).astype(BF16)
        f_buf[:, SPAN:] = (pair[32:] * scale).astype(BF16)
        copy = pltpu.make_async_copy(f_buf, gf_ref, f_sem.at[0])
        copy.start()
        copies.append(copy)

    for j in range(chunks):
        cols = slice(j * width, (j + 1) * width)
        place = (j ^ (TURN_BACK // count)) * count
        rows = got_ref[place:place + count, 0:32, :].reshape(width, SPAN)
        pair = jnp.transpose(rows).astype(F32)
        mixed = mixed_ref[:, cols] + jnp.where(kind == 2, pair, 0.0)
        series = series_ref[:, cols] + jnp.where(kind == 1, pair, 0.0)
        mixed = mixed.astype(BF16).astype(F32)
        series = series.astype(BF16).astype(F32)
        q_buf[:, cols] = (c_ref[:, cols].astype(F32) * mixed).astype(BF16)
        k_buf[:, cols] = (series * v_ref[:, cols].astype(F32)).astype(BF16)
        v_buf[:, cols] = (series * k_ref[:, cols].astype(F32)).astype(BF16)
        for i, (buf, ref) in enumerate(((q_buf, gq_ref), (k_buf, gk_ref), (v_buf, gv_ref))):
            copy = pltpu.make_async_copy(buf.at[:, cols], ref.at[:, cols], sems.at[i, j])
            copy.start()
            copies.append(copy)
        if j == 1:
            filter_taps()
    for copy in copies:
        copy.wait()


SMEM = pl.BlockSpec(memory_space=pltpu.SMEM)
VMEM = pl.BlockSpec(memory_space=pltpu.VMEM)
HBM = pl.BlockSpec(memory_space=pltpu.HBM)
ANY = pl.BlockSpec(memory_space=pl.ANY)
DMA = pltpu.SemaphoreType.DMA


def params(mebibytes=32):
    return pltpu.CompilerParams(vmem_limit_bytes=mebibytes * 1024 * 1024)


def cost(flops, moved):
    return pl.CostEstimate(flops=int(flops), bytes_accessed=int(moved), transcendentals=0)


def per_device(query, key, value, cotangent, filter_taps, span_slot, doc_lengths):
    parts = lax.axis_size("ctx")
    tokens, width = query.shape
    area = tokens * width
    pairs = parts - doc_lengths.shape[1]
    scale = float(tokens * parts * lax.axis_size("dp")) ** (-0.5)
    forward, inverse = transforms()

    def constant(matrix, axis):
        return jnp.asarray(np.concatenate(split_bf16(matrix), axis))

    fwd = constant(forward[:, :SPAN], 1)
    fwd_t = constant(forward[:, :SPAN].T, 0)
    inv = constant(inverse[:SPAN], 0)
    inv_t = constant(inverse[:SPAN].T, 1)
    tap_t = constant(np.roll(forward, -SPAN, 1).T, 0)
    lag_t = constant(np.roll(inverse, SPAN, 0).T, 1)
    core_swap = [(0, 1), (1, 0)]
    side_swap = [(c, c ^ 16) for c in range(parts)]
    cross_swap = [(c, c ^ 17) for c in range(parts)]
    next_swap = [(c, c ^ 1) for c in range(parts)]
    steps = width // 256
    taps_rows = filter_taps.T

    def exchange(array, turn):
        order = [[k ^ turn for k in range(parts)]]
        return lax.all_to_all(
            array, "ctx", split_axis=0, concat_axis=0, axis_index_groups=order, tiled=True
        )

    chunk = jax.ShapeDtypeStruct((parts, 40, SPAN), BF16)
    out = pl.pallas_call(
        send_kernel,
        out_shape=chunk,
        in_specs=[HBM] * 7,
        out_specs=HBM,
        scratch_shapes=[
            pltpu.SMEM(span_slot.shape, jnp.int32),
            pltpu.SMEM(doc_lengths.shape, jnp.int32),
            pltpu.VMEM(taps_rows.shape, BF16),
        ] + [pltpu.VMEM((tokens, width), BF16)] * 4 + [
            pltpu.VMEM(chunk.shape, BF16), DMA((3,)), DMA((4, 2)), DMA((2,)),
        ],
        compiler_params=params(60),
        cost_estimate=cost(2 * area, 8 * area),
        name="send",
    )(span_slot, doc_lengths, taps_rows, query, key, value, cotangent)
    got = exchange(out, TURN_OUT)

    give = pl.pallas_call(
        partial_kernel,
        out_shape=jax.ShapeDtypeStruct((4, parts * 8, SPAN), BF16),
        in_specs=[VMEM] * 6,
        out_specs=VMEM,
        compiler_params=params(),
        cost_estimate=cost(2e9, 10 * area),
        name="partial_taps",
    )(query, key, value, cotangent, fwd, inv)
    taken = lax.ppermute(give, "dp", core_swap)
    quarter = jax.ShapeDtypeStruct((parts * 8, SPAN), BF16)
    keep, side, near, cross = pl.pallas_call(
        share_kernel,
        out_shape=(jax.ShapeDtypeStruct(quarter.shape, F32), quarter, quarter, quarter),
        in_specs=[VMEM, VMEM],
        out_specs=(VMEM,) * 4,
        compiler_params=params(),
        cost_estimate=cost(area, 3 * area),
        name="share",
    )(give, taken)
    table, tap_spec = pl.pallas_call(
        tables_kernel,
        out_shape=(
            jax.ShapeDtypeStruct((3, 2 * pairs), jnp.int32),
            jax.ShapeDtypeStruct((32, PTS), F32),
        ),
        in_specs=[SMEM, SMEM, VMEM, VMEM, ANY],
        out_specs=(SMEM, VMEM),
        scratch_shapes=[pltpu.SMEM((parts,), jnp.int32)],
        compiler_params=params(),
        cost_estimate=cost(area, area),
        name="tables",
    )(span_slot, doc_lengths, taps_rows, tap_t, give)
    side = lax.ppermute(side, "ctx", side_swap)
    near = lax.ppermute(near, "ctx", next_swap)
    cross = lax.ppermute(cross, "ctx", cross_swap)

    back = pl.pallas_call(
        pair_kernel,
        out_shape=jax.ShapeDtypeStruct((parts, 32, SPAN), BF16),
        in_specs=[SMEM] + [VMEM] * 4,
        out_specs=VMEM,
        compiler_params=params(),
        cost_estimate=cost(1e9, 8 * area),
        name="pair",
    )(table, got, tap_spec, fwd_t, inv_t)
    back = pl.pallas_call(
        load_kernel,
        out_shape=chunk,
        in_specs=[VMEM] * 5,
        out_specs=HBM,
        scratch_shapes=[pltpu.VMEM(chunk.shape, BF16), DMA((2,))],
        compiler_params=params(),
        cost_estimate=cost(area, 4 * area),
        name="load",
    )(back, keep, side, near, cross)
    landed = exchange(back, TURN_BACK)

    own = got[:, 32:40, :].reshape(parts * 8, SPAN)
    pair_taps, xs, gs = pl.pallas_call(
        pair_taps_kernel,
        out_shape=(jax.ShapeDtypeStruct((64, SPAN), BF16),)
        + (jax.ShapeDtypeStruct((PTS, width), F32),) * 2,
        in_specs=[SMEM] + [VMEM] * 8,
        out_specs=(VMEM,) * 3,
        compiler_params=params(),
        cost_estimate=cost(1e9, 6 * area),
        name="pair_taps",
    )(table, got, query, key, value, cotangent, fwd_t, fwd, lag_t)
    own = jnp.concatenate([own, lax.ppermute(own, "ctx", side_swap), pair_taps], 0)
    core = lax.ppermute(own, "dp", core_swap)
    mixed, series = pl.pallas_call(
        local_kernel,
        out_shape=(jax.ShapeDtypeStruct((tokens, width), F32),) * 2,
        in_specs=[VMEM] * 6,
        out_specs=(VMEM, VMEM),
        compiler_params=params(),
        cost_estimate=cost(3e9, 20 * area),
        name="local",
    )(own, core, xs, gs, fwd, inv)

    result = jax.ShapeDtypeStruct((tokens, width), BF16)
    *grads, grad_filter = pl.pallas_call(
        functools.partial(finish_kernel, scale),
        out_shape=(result,) * 3 + (jax.ShapeDtypeStruct((32, PTS), BF16),),
        in_specs=[SMEM] + [VMEM] * 8,
        out_specs=(HBM,) * 4,
        scratch_shapes=[pltpu.VMEM((tokens, width), BF16)] * 3
        + [pltpu.VMEM((32, PTS), BF16), DMA((3, steps)), DMA((1,))],
        compiler_params=params(),
        cost_estimate=cost(10 * area, 20 * area),
        name="finish",
    )(table, landed, mixed, series, key, value, cotangent, own, core)
    return (*grads, grad_filter.T)


def solution(mesh):
    return jax.shard_map(
        per_device,
        mesh=mesh,
        in_specs=(
            P(("dp", "ctx"), "ch"),
            P(("dp", "ctx"), "ch"),
            P(("dp", "ctx"), "ch"),
            P(("dp", "ctx"), "ch"),
            P(None, ("ch", "ctx")),
            P("dp", None),
            P("dp", None),
        ),
        out_specs=(
            P(("dp", "ctx"), "ch"),
            P(("dp", "ctx"), "ch"),
            P(("dp", "ctx"), "ch"),
            P(None, ("ch", "ctx")),
        ),
        check_vma=False,
    )
```

```python
import functools

import jax
import jax.numpy as jnp
import numpy as np
from jax import lax
from jax.experimental import pallas as pl
from jax.experimental.pallas import tpu as pltpu
from jax.sharding import PartitionSpec as P

SPAN = 128
PTS = 2 * SPAN
QUARTER = SPAN // 4
BLOCK = 1024
TURN_OUT, TURN_BACK = 26, 24
F32, BF16 = jnp.float32, jnp.bfloat16


def split_bf16(matrix):
    high = matrix.astype(BF16)
    low = (matrix - high.astype(np.float64)).astype(BF16)
    return high, low


def transforms():
    freq = np.arange(SPAN)[:, None]
    point = np.arange(PTS)[None, :]
    angle = 2 * np.pi * ((freq * point) % PTS) / PTS
    real, imag = np.cos(angle), -np.sin(angle)
    imag[0] = np.where(np.arange(PTS) % 2 == 0, 1.0, -1.0)
    forward = np.concatenate([real, imag], 0)
    weight = np.full((PTS, 1), 2.0 / PTS)
    weight[0], weight[SPAN] = 1.0 / PTS, 1.0 / PTS
    inverse = (forward * weight).T
    return forward, inverse


def dot(a, b, dims=((1,), (0,))):
    return lax.dot_general(a, b, (dims, ((), ())), preferred_element_type=F32)


def halves(x):
    high = x.astype(BF16)
    return high, (x - high.astype(F32)).astype(BF16)


def spectrum_left(both, x):
    return dot(both, jnp.concatenate([x, x], 0))


def spectrum_right(x, both):
    return dot(jnp.concatenate([x, x], 1), both)


def invert_left(both, spec):
    s_high, s_low = halves(spec)
    main = dot(both, s_high)
    return main[:SPAN] + (main[SPAN:] + dot(both[:SPAN], s_low))


def invert_right(spec, both):
    s_high, s_low = halves(spec)
    main = dot(s_high, both)
    count = both.shape[1] // 2
    return main[:, :count] + (main[:, count:] + dot(s_low, both[:, :count]))


def multiply(ar, ai, br, bi, zero, sign):
    b_im = sign * jnp.where(zero, 0.0, bi)
    b_second = jnp.where(zero, bi, br)
    return ar * br - ai * b_im, ai * b_second + ar * b_im


def swap_blocks(parts):
    axis = parts[0].ndim - 1
    block = lax.broadcasted_iota(jnp.int32, parts[0].shape, axis) // QUARTER
    result = []
    for t in range(4):
        total = parts[t]
        for b in range(4):
            if b != t:
                moved = pltpu.roll(parts[b], (QUARTER * (b - t)) % SPAN, axis)
                total = jnp.where(block == b, moved, total)
        result.append(total)
    return result


def own_kind(slot_ref, len_ref):
    span = slot_ref[0, lax.axis_index("ctx")]

    def step(d, carry):
        pos, kind = carry
        length = len_ref[0, d]
        two = length == 2
        kind = jnp.where(two & (span == pos), 1, kind)
        kind = jnp.where(two & (span == pos + 1), 2, kind)
        return pos + length, kind

    zero = jnp.int32(0)
    return lax.fori_loop(0, len_ref.shape[1], step, (zero, zero), unroll=True)[1]


def send_kernel(
    slot_hbm, len_hbm, taps_hbm, q_hbm, k_hbm, v_hbm, c_hbm, out_hbm,
    slot_ref, len_ref, taps_ref, q_buf, k_buf, v_buf, c_buf, out_buf,
    small_sem, in_sem, out_sem,
):
    chunks = out_sem.shape[0]
    width = q_buf.shape[1] // chunks
    count = out_buf.shape[0] // chunks
    small = [
        pltpu.make_async_copy(src, dst, small_sem.at[i])
        for i, (src, dst) in enumerate(
            ((slot_hbm, slot_ref), (len_hbm, len_ref), (taps_hbm, taps_ref))
        )
    ]
    small[0].start()
    small[1].start()
    wide = []
    for j in range(chunks):
        cols = pl.ds(j * width, width)
        wide.append([
            pltpu.make_async_copy(src.at[:, cols], dst.at[:, cols], in_sem.at[i, j])
            for i, (src, dst) in enumerate(
                ((k_hbm, k_buf), (v_hbm, v_buf), (c_hbm, c_buf), (q_hbm, q_buf))
            )
        ])
        for copy in wide[-1]:
            copy.start()
        if j == 0:
            small[2].start()
    small[0].wait()
    small[1].wait()
    first = own_kind(slot_ref, len_ref) == 1
    small[2].wait()
    taps = taps_ref[:, 0:SPAN].astype(F32)
    quarters = swap_blocks([taps[8 * b:8 * b + 8] for b in range(4)])
    core = lax.axis_index("dp") == 0
    outs = []
    for j in range(chunks):
        for copy in wide[j]:
            copy.wait()
        cols = slice(j * width, (j + 1) * width)
        a = jnp.where(first, k_buf[:, cols].astype(F32), c_buf[:, cols].astype(F32))
        b = jnp.where(first, v_buf[:, cols].astype(F32), q_buf[:, cols].astype(F32))
        series = jnp.transpose((a * b).astype(BF16)).reshape(count, 32, SPAN)
        far = int(2 * j >= chunks)
        mine = jnp.where(core, quarters[far], quarters[2 + far]).astype(BF16)
        for piece in range(0, count, 2):
            rows = pl.ds((j * count + piece) ^ TURN_OUT, 2)
            out_buf[rows, 0:32, :] = series[piece:piece + 2]
            out_buf[rows, 32:40, :] = jnp.broadcast_to(mine[None], (2, 8, SPAN))
        rows = pl.ds((j * count) ^ (TURN_OUT // count * count), count)
        out = pltpu.make_async_copy(out_buf.at[rows], out_hbm.at[rows], out_sem.at[j])
        out.start()
        outs.append(out)
    for out in outs:
        out.wait()


def partial_kernel(
    q_ref, k_ref, v_ref, c_ref, fwd, inv, give_ref
):
    blocks = q_ref.shape[1] // BLOCK
    count = BLOCK // 32
    zero = lax.broadcasted_iota(jnp.int32, (SPAN, BLOCK), 0) == 0
    for j in range(blocks):
        cols = slice(j * BLOCK, (j + 1) * BLOCK)
        x = (k_ref[:, cols].astype(F32) * v_ref[:, cols].astype(F32)).astype(BF16)
        g = (c_ref[:, cols].astype(F32) * q_ref[:, cols].astype(F32)).astype(BF16)
        xs = spectrum_left(fwd[...], x)
        gs = spectrum_left(fwd[...], g)
        pr, pi = multiply(gs[:SPAN], gs[SPAN:], xs[:SPAN], xs[SPAN:], zero, -1.0)
        taps = invert_left(inv[...], jnp.concatenate([pr, pi], 0))
        rows = jnp.transpose(taps).reshape(count, 4, 8, SPAN)
        quarters = swap_blocks([rows[:, b] for b in range(4)])
        for t in range(4):
            packed = quarters[t].reshape(count * 8, SPAN).astype(BF16)
            give_ref[t, j * count * 8:(j + 1) * count * 8, :] = packed


def tables_kernel(
    slot_ref, len_ref, taps_ref, tap, after_ref, table_ref, spec_ref, inverse_ref
):
    del after_ref
    spec_ref[...] = spectrum_right(taps_ref[...], tap[...])

    slots = slot_ref.shape[1]

    def fill(r, carry):
        inverse_ref[slot_ref[0, r]] = r
        return carry

    lax.fori_loop(0, slots, fill, 0, unroll=True)

    def step(d, carry):
        pos, count = carry
        length = len_ref[0, d]
        table_ref[0, count] = inverse_ref[pos]
        table_ref[1, count] = inverse_ref[jnp.minimum(pos + 1, slots - 1)]
        return pos + length, count + length - 1

    zero = jnp.int32(0)
    lax.fori_loop(0, len_ref.shape[1], step, (zero, zero), unroll=True)
    table_ref[2, 0] = own_kind(slot_ref, len_ref)


def share_kernel(own_ref, other_ref, keep_ref, side_ref, next_ref, cross_ref):
    ctx = lax.axis_index("ctx")
    far, odd = ctx // 16, ctx % 2

    def total(t):
        return own_ref[t].astype(F32) + other_ref[t].astype(F32)

    keep_ref[...] = total(2 * far + odd)
    side_ref[...] = total(2 * (1 - far) + odd).astype(BF16)
    next_ref[...] = total(2 * far + 1 - odd).astype(BF16)
    cross_ref[...] = total(2 * (1 - far) + 1 - odd).astype(BF16)


def pair_spectra(table_ref, got_ref, fwd):
    pairs = table_ref.shape[1] // 2
    rows = [got_ref[table_ref[k, p] ^ TURN_OUT, 0:32, :] for k in range(2) for p in range(pairs)]
    spec = spectrum_right(jnp.concatenate(rows, 0), fwd[...])
    return spec.reshape(2, pairs, 32, PTS)


def pair_kernel(
    table_ref, got_ref, spec_ref, fwd, inv, out_ref
):
    slots, pairs = got_ref.shape[0], table_ref.shape[1] // 2
    hr, hi = spec_ref[:, :SPAN], spec_ref[:, SPAN:]
    zero = lax.broadcasted_iota(jnp.int32, hr.shape, 1) == 0
    spec = pair_spectra(table_ref, got_ref, fwd)
    out_ref[...] = jnp.zeros((slots, 32, SPAN), BF16)
    for k in range(2):
        sr, si = spec[k, :, :, :SPAN], spec[k, :, :, SPAN:]
        pr, pi = multiply(sr, si, hr[None], hi[None], zero[None], 1.0 if k == 0 else -1.0)
        both = jnp.concatenate([pr, pi], 2).reshape(pairs * 32, PTS)
        result = invert_right(both, inv[...]).astype(BF16)
        for p in range(pairs):
            out_ref[table_ref[1 - k, p] ^ TURN_BACK] = result[32 * p:32 * p + 32]


def load_kernel(
    pair_ref, keep_ref, side_ref, next_ref, cross_ref, out_hbm, out_buf, sems
):
    slots = pair_ref.shape[0]
    half = slots // 2
    copies = []
    for h in range(2):
        source = slice(h * half * 8, (h + 1) * half * 8)
        near = keep_ref[source] + side_ref[source].astype(F32)
        near = near + (next_ref[source].astype(F32) + cross_ref[source].astype(F32))
        near = near.astype(BF16).reshape(half, 8, SPAN)
        start = (h * half) ^ (TURN_BACK // half * half)
        rows = slice(start, start + half)
        out_buf[rows, 0:32, :] = pair_ref[rows]
        for piece in range(0, half, 8):
            place = (h * half + piece) ^ TURN_BACK
            out_buf[place:place + 8, 32:40, :] = near[piece:piece + 8]
        copy = pltpu.make_async_copy(out_buf.at[rows], out_hbm.at[rows], sems.at[h])
        copy.start()
        copies.append(copy)
    for copy in copies:
        copy.wait()


def pair_taps_kernel(
    table_ref, got_ref, q_ref, k_ref, v_ref, c_ref, fwd, own_fwd, lag,
    out_ref, xs_ref, gs_ref,
):
    for j in range(q_ref.shape[1] // BLOCK):
        cols = slice(j * BLOCK, (j + 1) * BLOCK)
        x = (k_ref[:, cols].astype(F32) * v_ref[:, cols].astype(F32)).astype(BF16)
        g = (c_ref[:, cols].astype(F32) * q_ref[:, cols].astype(F32)).astype(BF16)
        xs_ref[:, cols] = spectrum_left(own_fwd[...], x)
        gs_ref[:, cols] = spectrum_left(own_fwd[...], g)
    spec = pair_spectra(table_ref, got_ref, fwd)
    zero = lax.broadcasted_iota(jnp.int32, (1, 32, SPAN), 2) == 0
    xs, gs = spec[0], spec[1]
    tr, ti = multiply(
        gs[:, :, :SPAN], gs[:, :, SPAN:], xs[:, :, :SPAN], xs[:, :, SPAN:], zero, -1.0
    )
    both = jnp.concatenate([jnp.sum(tr, 0), jnp.sum(ti, 0)], 1)
    taps = invert_right(both, lag[...]).astype(BF16)
    out_ref[0:32, :] = taps[:, :SPAN]
    out_ref[32:64, :] = taps[:, SPAN:]


def local_kernel(
    own_ref, core_ref, xs_ref, gs_ref, fwd, inv, mixed_ref, series_ref
):
    blocks = xs_ref.shape[1] // BLOCK
    count = BLOCK // 32
    dp, far = lax.axis_index("dp"), lax.axis_index("ctx") // 16
    zero = lax.broadcasted_iota(jnp.int32, (SPAN, BLOCK), 0) == 0
    nt = ((1,), (1,))
    for j in range(blocks):
        cols = slice(j * BLOCK, (j + 1) * BLOCK)
        xs, gs = xs_ref[:, cols], gs_ref[:, cols]

        def rows(ref, start):
            blocks = range(j * BLOCK // 64, (j + 1) * BLOCK // 64)
            places = [start + 16 * (b ^ (TURN_OUT // 2)) for b in blocks]
            return jnp.concatenate([ref[p:p + 16, :].astype(F32) for p in places], 0)

        own, side = rows(own_ref, 0), rows(own_ref, 256)
        core, cross = rows(core_ref, 0), rows(core_ref, 256)
        quarters = []
        for t in range(4):
            here = jnp.where(far == t % 2, own, side)
            there = jnp.where(far == t % 2, core, cross)
            quarters.append(jnp.where(dp == t // 2, here, there).reshape(count, 8, SPAN))
        taps = jnp.concatenate(swap_blocks(quarters), 1).reshape(BLOCK, SPAN).astype(BF16)
        hs = dot(fwd[...], jnp.concatenate([taps, taps], 1), nt)
        hr, hi = hs[:SPAN], hs[SPAN:]
        mr, mi = multiply(xs[:SPAN], xs[SPAN:], hr, hi, zero, 1.0)
        spec = jnp.concatenate([mr, mi], 0)
        mixed_ref[:, cols] = invert_left(inv[...], spec)
        sr, si = multiply(gs[:SPAN], gs[SPAN:], hr, hi, zero, -1.0)
        spec = jnp.concatenate([sr, si], 0)
        series_ref[:, cols] = invert_left(inv[...], spec)


def finish_kernel(
    scale, table_ref, got_ref, mixed_ref, series_ref, k_ref, v_ref, c_ref, own_ref, core_ref,
    gq_ref, gk_ref, gv_ref, gf_ref, q_buf, k_buf, v_buf, f_buf, sems, f_sem,
):
    chunks = sems.shape[1]
    width = q_buf.shape[1] // chunks
    slots = got_ref.shape[0]
    count = slots // chunks
    kind = table_ref[2, 0]
    copies = []

    def filter_taps():
        quarters = []
        for t in range(4):
            sources = [s ^ TURN_BACK for s in range(slots) if 2 * (s // 16) + s % 2 == t]
            quarters.append(sum(got_ref[s, 32:40, :].astype(F32) for s in sources))
        near = jnp.concatenate(swap_blocks(quarters), 0)
        pair = own_ref[512:576, :].astype(F32) + core_ref[512:576, :].astype(F32)
        f_buf[:, :SPAN] = ((near + pair[:32]) * scale).astype(BF16)
        f_buf[:, SPAN:] = (pair[32:] * scale).astype(BF16)
        copy = pltpu.make_async_copy(f_buf, gf_ref, f_sem.at[0])
        copy.start()
        copies.append(copy)

    for j in range(chunks):
        cols = slice(j * width, (j + 1) * width)
        place = (j ^ (TURN_BACK // count)) * count
        rows = got_ref[place:place + count, 0:32, :].reshape(width, SPAN)
        pair = jnp.transpose(rows).astype(F32)
        mixed = mixed_ref[:, cols] + jnp.where(kind == 2, pair, 0.0)
        series = series_ref[:, cols] + jnp.where(kind == 1, pair, 0.0)
        mixed = mixed.astype(BF16).astype(F32)
        series = series.astype(BF16).astype(F32)
        q_buf[:, cols] = (c_ref[:, cols].astype(F32) * mixed).astype(BF16)
        k_buf[:, cols] = (series * v_ref[:, cols].astype(F32)).astype(BF16)
        v_buf[:, cols] = (series * k_ref[:, cols].astype(F32)).astype(BF16)
        for i, (buf, ref) in enumerate(((q_buf, gq_ref), (k_buf, gk_ref), (v_buf, gv_ref))):
            copy = pltpu.make_async_copy(buf.at[:, cols], ref.at[:, cols], sems.at[i, j])
            copy.start()
            copies.append(copy)
        if j == 1:
            filter_taps()
    for copy in copies:
        copy.wait()


SMEM = pl.BlockSpec(memory_space=pltpu.SMEM)
VMEM = pl.BlockSpec(memory_space=pltpu.VMEM)
HBM = pl.BlockSpec(memory_space=pltpu.HBM)
ANY = pl.BlockSpec(memory_space=pl.ANY)
DMA = pltpu.SemaphoreType.DMA


def params(mebibytes=32):
    return pltpu.CompilerParams(vmem_limit_bytes=mebibytes * 1024 * 1024)


def cost(flops, moved):
    return pl.CostEstimate(flops=int(flops), bytes_accessed=int(moved), transcendentals=0)


def per_device(query, key, value, cotangent, filter_taps, span_slot, doc_lengths):
    parts = lax.axis_size("ctx")
    tokens, width = query.shape
    area = tokens * width
    pairs = parts - doc_lengths.shape[1]
    scale = float(tokens * parts * lax.axis_size("dp")) ** (-0.5)
    forward, inverse = transforms()

    def constant(matrix, axis):
        return jnp.asarray(np.concatenate(split_bf16(matrix), axis))

    fwd = constant(forward[:, :SPAN], 1)
    fwd_t = constant(forward[:, :SPAN].T, 0)
    inv = constant(inverse[:SPAN], 0)
    inv_t = constant(inverse[:SPAN].T, 1)
    tap_t = constant(np.roll(forward, -SPAN, 1).T, 0)
    lag_t = constant(np.roll(inverse, SPAN, 0).T, 1)
    core_swap = [(0, 1), (1, 0)]
    side_swap = [(c, c ^ 16) for c in range(parts)]
    cross_swap = [(c, c ^ 17) for c in range(parts)]
    next_swap = [(c, c ^ 1) for c in range(parts)]
    steps = width // 256
    taps_rows = filter_taps.T

    def exchange(array, turn):
        order = [[k ^ turn for k in range(parts)]]
        return lax.all_to_all(
            array, "ctx", split_axis=0, concat_axis=0, axis_index_groups=order, tiled=True
        )

    chunk = jax.ShapeDtypeStruct((parts, 40, SPAN), BF16)
    out = pl.pallas_call(
        send_kernel,
        out_shape=chunk,
        in_specs=[HBM] * 7,
        out_specs=HBM,
        scratch_shapes=[
            pltpu.SMEM(span_slot.shape, jnp.int32),
            pltpu.SMEM(doc_lengths.shape, jnp.int32),
            pltpu.VMEM(taps_rows.shape, BF16),
        ] + [pltpu.VMEM((tokens, width), BF16)] * 4 + [
            pltpu.VMEM(chunk.shape, BF16), DMA((3,)), DMA((4, 2)), DMA((2,)),
        ],
        compiler_params=params(60),
        cost_estimate=cost(2 * area, 8 * area),
        name="send",
    )(span_slot, doc_lengths, taps_rows, query, key, value, cotangent)
    got = exchange(out, TURN_OUT)

    give = pl.pallas_call(
        partial_kernel,
        out_shape=jax.ShapeDtypeStruct((4, parts * 8, SPAN), BF16),
        in_specs=[VMEM] * 6,
        out_specs=VMEM,
        compiler_params=params(),
        cost_estimate=cost(2e9, 10 * area),
        name="partial_taps",
    )(query, key, value, cotangent, fwd, inv)
    taken = lax.ppermute(give, "dp", core_swap)
    quarter = jax.ShapeDtypeStruct((parts * 8, SPAN), BF16)
    keep, side, near, cross = pl.pallas_call(
        share_kernel,
        out_shape=(jax.ShapeDtypeStruct(quarter.shape, F32), quarter, quarter, quarter),
        in_specs=[VMEM, VMEM],
        out_specs=(VMEM,) * 4,
        compiler_params=params(),
        cost_estimate=cost(area, 3 * area),
        name="share",
    )(give, taken)
    table, tap_spec = pl.pallas_call(
        tables_kernel,
        out_shape=(
            jax.ShapeDtypeStruct((3, 2 * pairs), jnp.int32),
            jax.ShapeDtypeStruct((32, PTS), F32),
        ),
        in_specs=[SMEM, SMEM, VMEM, VMEM, ANY],
        out_specs=(SMEM, VMEM),
        scratch_shapes=[pltpu.SMEM((parts,), jnp.int32)],
        compiler_params=params(),
        cost_estimate=cost(area, area),
        name="tables",
    )(span_slot, doc_lengths, taps_rows, tap_t, give)
    side = lax.ppermute(side, "ctx", side_swap)
    near = lax.ppermute(near, "ctx", next_swap)
    cross = lax.ppermute(cross, "ctx", cross_swap)

    back = pl.pallas_call(
        pair_kernel,
        out_shape=jax.ShapeDtypeStruct((parts, 32, SPAN), BF16),
        in_specs=[SMEM] + [VMEM] * 4,
        out_specs=VMEM,
        compiler_params=params(),
        cost_estimate=cost(1e9, 8 * area),
        name="pair",
    )(table, got, tap_spec, fwd_t, inv_t)
    back = pl.pallas_call(
        load_kernel,
        out_shape=chunk,
        in_specs=[VMEM] * 5,
        out_specs=HBM,
        scratch_shapes=[pltpu.VMEM(chunk.shape, BF16), DMA((2,))],
        compiler_params=params(),
        cost_estimate=cost(area, 4 * area),
        name="load",
    )(back, keep, cross, near, side)
    landed = exchange(back, TURN_BACK)

    own = got[:, 32:40, :].reshape(parts * 8, SPAN)
    pair_taps, xs, gs = pl.pallas_call(
        pair_taps_kernel,
        out_shape=(jax.ShapeDtypeStruct((64, SPAN), BF16),)
        + (jax.ShapeDtypeStruct((PTS, width), F32),) * 2,
        in_specs=[SMEM] + [VMEM] * 8,
        out_specs=(VMEM,) * 3,
        compiler_params=params(),
        cost_estimate=cost(1e9, 6 * area),
        name="pair_taps",
    )(table, got, query, key, value, cotangent, fwd_t, fwd, lag_t)
    own = jnp.concatenate([own, lax.ppermute(own, "ctx", side_swap), pair_taps], 0)
    core = lax.ppermute(own, "dp", core_swap)
    mixed, series = pl.pallas_call(
        local_kernel,
        out_shape=(jax.ShapeDtypeStruct((tokens, width), F32),) * 2,
        in_specs=[VMEM] * 6,
        out_specs=(VMEM, VMEM),
        compiler_params=params(),
        cost_estimate=cost(3e9, 20 * area),
        name="local",
    )(own, core, xs, gs, fwd, inv)

    result = jax.ShapeDtypeStruct((tokens, width), BF16)
    *grads, grad_filter = pl.pallas_call(
        functools.partial(finish_kernel, scale),
        out_shape=(result,) * 3 + (jax.ShapeDtypeStruct((32, PTS), BF16),),
        in_specs=[SMEM] + [VMEM] * 8,
        out_specs=(HBM,) * 4,
        scratch_shapes=[pltpu.VMEM((tokens, width), BF16)] * 3
        + [pltpu.VMEM((32, PTS), BF16), DMA((3, steps)), DMA((1,))],
        compiler_params=params(),
        cost_estimate=cost(10 * area, 20 * area),
        name="finish",
    )(table, landed, mixed, series, key, value, cotangent, own, core)
    return (*grads, grad_filter.T)


def solution(mesh):
    return jax.shard_map(
        per_device,
        mesh=mesh,
        in_specs=(
            P(("dp", "ctx"), "ch"),
            P(("dp", "ctx"), "ch"),
            P(("dp", "ctx"), "ch"),
            P(("dp", "ctx"), "ch"),
            P(None, ("ch", "ctx")),
            P("dp", None),
            P("dp", None),
        ),
        out_specs=(
            P(("dp", "ctx"), "ch"),
            P(("dp", "ctx"), "ch"),
            P(("dp", "ctx"), "ch"),
            P(None, ("ch", "ctx")),
        ),
        check_vma=False,
    )
```

```python
import functools

import jax
import jax.numpy as jnp
import numpy as np
from jax import lax
from jax.experimental import pallas as pl
from jax.experimental.pallas import tpu as pltpu
from jax.sharding import PartitionSpec as P

SPAN = 128
PTS = 2 * SPAN
QUARTER = SPAN // 4
BLOCK = 1024
TURN_OUT, TURN_BACK = 26, 24
F32, BF16 = jnp.float32, jnp.bfloat16


def split_bf16(matrix):
    high = matrix.astype(BF16)
    low = (matrix - high.astype(np.float64)).astype(BF16)
    return high, low


def transforms():
    freq = np.arange(SPAN)[:, None]
    point = np.arange(PTS)[None, :]
    angle = 2 * np.pi * ((freq * point) % PTS) / PTS
    real, imag = np.cos(angle), -np.sin(angle)
    imag[0] = np.where(np.arange(PTS) % 2 == 0, 1.0, -1.0)
    forward = np.concatenate([real, imag], 0)
    weight = np.full((PTS, 1), 2.0 / PTS)
    weight[0], weight[SPAN] = 1.0 / PTS, 1.0 / PTS
    inverse = (forward * weight).T
    return forward, inverse


def dot(a, b, dims=((1,), (0,))):
    return lax.dot_general(a, b, (dims, ((), ())), preferred_element_type=F32)


def halves(x):
    high = x.astype(BF16)
    return high, (x - high.astype(F32)).astype(BF16)


def spectrum_left(both, x):
    return dot(both, jnp.concatenate([x, x], 0))


def spectrum_right(x, both):
    return dot(jnp.concatenate([x, x], 1), both)


def invert_left(both, spec):
    s_high, s_low = halves(spec)
    main = dot(both, s_high)
    return main[:SPAN] + (main[SPAN:] + dot(both[:SPAN], s_low))


def invert_right(spec, both):
    s_high, s_low = halves(spec)
    main = dot(s_high, both)
    count = both.shape[1] // 2
    return main[:, :count] + (main[:, count:] + dot(s_low, both[:, :count]))


def multiply(ar, ai, br, bi, zero, sign):
    b_im = sign * jnp.where(zero, 0.0, bi)
    b_second = jnp.where(zero, bi, br)
    return ar * br - ai * b_im, ai * b_second + ar * b_im


def swap_blocks(parts):
    axis = parts[0].ndim - 1
    block = lax.broadcasted_iota(jnp.int32, parts[0].shape, axis) // QUARTER
    result = []
    for t in range(4):
        total = parts[t]
        for b in range(4):
            if b != t:
                moved = pltpu.roll(parts[b], (QUARTER * (b - t)) % SPAN, axis)
                total = jnp.where(block == b, moved, total)
        result.append(total)
    return result


def own_kind(slot_ref, len_ref):
    span = slot_ref[0, lax.axis_index("ctx")]

    def step(d, carry):
        pos, kind = carry
        length = len_ref[0, d]
        two = length == 2
        kind = jnp.where(two & (span == pos), 1, kind)
        kind = jnp.where(two & (span == pos + 1), 2, kind)
        return pos + length, kind

    zero = jnp.int32(0)
    return lax.fori_loop(0, len_ref.shape[1], step, (zero, zero), unroll=True)[1]


def send_kernel(
    slot_hbm, len_hbm, taps_hbm, q_hbm, k_hbm, v_hbm, c_hbm, out_hbm,
    slot_ref, len_ref, taps_ref, q_buf, k_buf, v_buf, c_buf, out_buf,
    small_sem, in_sem, out_sem,
):
    chunks = out_sem.shape[0]
    width = q_buf.shape[1] // chunks
    count = out_buf.shape[0] // chunks
    small = [
        pltpu.make_async_copy(src, dst, small_sem.at[i])
        for i, (src, dst) in enumerate(
            ((slot_hbm, slot_ref), (len_hbm, len_ref), (taps_hbm, taps_ref))
        )
    ]
    small[0].start()
    small[1].start()
    wide = []
    for j in range(chunks):
        cols = pl.ds(j * width, width)
        wide.append([
            pltpu.make_async_copy(src.at[:, cols], dst.at[:, cols], in_sem.at[i, j])
            for i, (src, dst) in enumerate(
                ((k_hbm, k_buf), (v_hbm, v_buf), (c_hbm, c_buf), (q_hbm, q_buf))
            )
        ])
        for copy in wide[-1]:
            copy.start()
        if j == 0:
            small[2].start()
    small[0].wait()
    small[1].wait()
    first = own_kind(slot_ref, len_ref) == 1
    small[2].wait()
    taps = taps_ref[:, 0:SPAN].astype(F32)
    quarters = swap_blocks([taps[8 * b:8 * b + 8] for b in range(4)])
    core = lax.axis_index("dp") == 0
    outs = []
    for j in range(chunks):
        for copy in wide[j]:
            copy.wait()
        cols = slice(j * width, (j + 1) * width)
        a = jnp.where(first, k_buf[:, cols].astype(F32), c_buf[:, cols].astype(F32))
        b = jnp.where(first, v_buf[:, cols].astype(F32), q_buf[:, cols].astype(F32))
        series = jnp.transpose((a * b).astype(BF16)).reshape(count, 32, SPAN)
        far = int(2 * j >= chunks)
        mine = jnp.where(core, quarters[far], quarters[2 + far]).astype(BF16)
        for piece in range(0, count, 2):
            rows = pl.ds((j * count + piece) ^ TURN_OUT, 2)
            out_buf[rows, 0:32, :] = series[piece:piece + 2]
            out_buf[rows, 32:40, :] = jnp.broadcast_to(mine[None], (2, 8, SPAN))
        rows = pl.ds((j * count) ^ (TURN_OUT // count * count), count)
        out = pltpu.make_async_copy(out_buf.at[rows], out_hbm.at[rows], out_sem.at[j])
        out.start()
        outs.append(out)
    for out in outs:
        out.wait()


def partial_kernel(
    q_ref, k_ref, v_ref, c_ref, fwd, inv, give_ref
):
    blocks = q_ref.shape[1] // BLOCK
    count = BLOCK // 32
    zero = lax.broadcasted_iota(jnp.int32, (SPAN, BLOCK), 0) == 0
    for j in range(blocks):
        cols = slice(j * BLOCK, (j + 1) * BLOCK)
        x = (k_ref[:, cols].astype(F32) * v_ref[:, cols].astype(F32)).astype(BF16)
        g = (c_ref[:, cols].astype(F32) * q_ref[:, cols].astype(F32)).astype(BF16)
        xs = spectrum_left(fwd[...], x)
        gs = spectrum_left(fwd[...], g)
        pr, pi = multiply(gs[:SPAN], gs[SPAN:], xs[:SPAN], xs[SPAN:], zero, -1.0)
        taps = invert_left(inv[...], jnp.concatenate([pr, pi], 0))
        rows = jnp.transpose(taps).reshape(count, 4, 8, SPAN)
        quarters = swap_blocks([rows[:, b] for b in range(4)])
        for t in range(4):
            packed = quarters[t].reshape(count * 8, SPAN).astype(BF16)
            give_ref[t, j * count * 8:(j + 1) * count * 8, :] = packed


def tables_kernel(
    slot_ref, len_ref, taps_ref, tap, after_ref, table_ref, spec_ref, inverse_ref
):
    del after_ref
    spec_ref[...] = spectrum_right(taps_ref[...], tap[...])

    slots = slot_ref.shape[1]

    def fill(r, carry):
        inverse_ref[slot_ref[0, r]] = r
        return carry

    lax.fori_loop(0, slots, fill, 0, unroll=True)

    def step(d, carry):
        pos, count = carry
        length = len_ref[0, d]
        table_ref[0, count] = inverse_ref[pos]
        table_ref[1, count] = inverse_ref[jnp.minimum(pos + 1, slots - 1)]
        return pos + length, count + length - 1

    zero = jnp.int32(0)
    lax.fori_loop(0, len_ref.shape[1], step, (zero, zero), unroll=True)
    table_ref[2, 0] = own_kind(slot_ref, len_ref)


def share_kernel(own_ref, other_ref, keep_ref, side_ref, next_ref, cross_ref):
    ctx = lax.axis_index("ctx")
    far, odd = ctx // 16, ctx % 2

    def total(t):
        return own_ref[t].astype(F32) + other_ref[t].astype(F32)

    keep_ref[...] = total(2 * far + odd)
    side_ref[...] = total(2 * (1 - far) + odd).astype(BF16)
    next_ref[...] = total(2 * far + 1 - odd).astype(BF16)
    cross_ref[...] = total(2 * (1 - far) + 1 - odd).astype(BF16)


def pair_spectra(table_ref, got_ref, fwd):
    pairs = table_ref.shape[1] // 2
    rows = [got_ref[table_ref[k, p] ^ TURN_OUT, 0:32, :] for k in range(2) for p in range(pairs)]
    spec = spectrum_right(jnp.concatenate(rows, 0), fwd[...])
    return spec.reshape(2, pairs, 32, PTS)


def pair_kernel(
    table_ref, got_ref, spec_ref, fwd, inv, out_ref
):
    slots, pairs = got_ref.shape[0], table_ref.shape[1] // 2
    hr, hi = spec_ref[:, :SPAN], spec_ref[:, SPAN:]
    zero = lax.broadcasted_iota(jnp.int32, hr.shape, 1) == 0
    spec = pair_spectra(table_ref, got_ref, fwd)
    out_ref[...] = jnp.zeros((slots, 32, SPAN), BF16)
    both = []
    for k in range(2):
        sr, si = spec[k, :, :, :SPAN], spec[k, :, :, SPAN:]
        pr, pi = multiply(sr, si, hr[None], hi[None], zero[None], 1.0 if k == 0 else -1.0)
        both.append(jnp.concatenate([pr, pi], 2).reshape(pairs * 32, PTS))
    result = invert_right(jnp.concatenate(both, 0), inv[...]).astype(BF16)
    for k in range(2):
        for p in range(pairs):
            row = 32 * (k * pairs + p)
            out_ref[table_ref[1 - k, p] ^ TURN_BACK] = result[row:row + 32]


def load_kernel(
    pair_ref, keep_ref, side_ref, next_ref, cross_ref, out_hbm, out_buf, sems
):
    slots = pair_ref.shape[0]
    half = slots // 2
    copies = []
    for h in range(2):
        source = slice(h * half * 8, (h + 1) * half * 8)
        near = keep_ref[source] + side_ref[source].astype(F32)
        near = near + (next_ref[source].astype(F32) + cross_ref[source].astype(F32))
        near = near.astype(BF16).reshape(half, 8, SPAN)
        start = (h * half) ^ (TURN_BACK // half * half)
        rows = slice(start, start + half)
        out_buf[rows, 0:32, :] = pair_ref[rows]
        for piece in range(0, half, 8):
            place = (h * half + piece) ^ TURN_BACK
            out_buf[place:place + 8, 32:40, :] = near[piece:piece + 8]
        copy = pltpu.make_async_copy(out_buf.at[rows], out_hbm.at[rows], sems.at[h])
        copy.start()
        copies.append(copy)
    for copy in copies:
        copy.wait()


def pair_taps_kernel(
    table_ref, got_ref, q_ref, k_ref, v_ref, c_ref, fwd, own_fwd, lag,
    out_ref, xs_ref, gs_ref,
):
    for j in range(q_ref.shape[1] // BLOCK):
        cols = slice(j * BLOCK, (j + 1) * BLOCK)
        x = (k_ref[:, cols].astype(F32) * v_ref[:, cols].astype(F32)).astype(BF16)
        g = (c_ref[:, cols].astype(F32) * q_ref[:, cols].astype(F32)).astype(BF16)
        xs_ref[:, cols] = spectrum_left(own_fwd[...], x)
        gs_ref[:, cols] = spectrum_left(own_fwd[...], g)
    spec = pair_spectra(table_ref, got_ref, fwd)
    zero = lax.broadcasted_iota(jnp.int32, (1, 32, SPAN), 2) == 0
    xs, gs = spec[0], spec[1]
    tr, ti = multiply(
        gs[:, :, :SPAN], gs[:, :, SPAN:], xs[:, :, :SPAN], xs[:, :, SPAN:], zero, -1.0
    )
    both = jnp.concatenate([jnp.sum(tr, 0), jnp.sum(ti, 0)], 1)
    taps = invert_right(both, lag[...]).astype(BF16)
    out_ref[0:32, :] = taps[:, :SPAN]
    out_ref[32:64, :] = taps[:, SPAN:]


def local_kernel(
    own_ref, core_ref, xs_ref, gs_ref, fwd, inv, mixed_ref, series_ref
):
    blocks = xs_ref.shape[1] // BLOCK
    count = BLOCK // 32
    dp, far = lax.axis_index("dp"), lax.axis_index("ctx") // 16
    zero = lax.broadcasted_iota(jnp.int32, (SPAN, BLOCK), 0) == 0
    nt = ((1,), (1,))
    for j in range(blocks):
        cols = slice(j * BLOCK, (j + 1) * BLOCK)
        xs, gs = xs_ref[:, cols], gs_ref[:, cols]

        def rows(ref, start):
            blocks = range(j * BLOCK // 64, (j + 1) * BLOCK // 64)
            places = [start + 16 * (b ^ (TURN_OUT // 2)) for b in blocks]
            return jnp.concatenate([ref[p:p + 16, :].astype(F32) for p in places], 0)

        own, side = rows(own_ref, 0), rows(own_ref, 256)
        core, cross = rows(core_ref, 0), rows(core_ref, 256)
        quarters = []
        for t in range(4):
            here = jnp.where(far == t % 2, own, side)
            there = jnp.where(far == t % 2, core, cross)
            quarters.append(jnp.where(dp == t // 2, here, there).reshape(count, 8, SPAN))
        taps = jnp.concatenate(swap_blocks(quarters), 1).reshape(BLOCK, SPAN).astype(BF16)
        hs = dot(fwd[...], jnp.concatenate([taps, taps], 1), nt)
        hr, hi = hs[:SPAN], hs[SPAN:]
        mr, mi = multiply(xs[:SPAN], xs[SPAN:], hr, hi, zero, 1.0)
        spec = jnp.concatenate([mr, mi], 0)
        mixed_ref[:, cols] = invert_left(inv[...], spec)
        sr, si = multiply(gs[:SPAN], gs[SPAN:], hr, hi, zero, -1.0)
        spec = jnp.concatenate([sr, si], 0)
        series_ref[:, cols] = invert_left(inv[...], spec)


def finish_kernel(
    scale, table_ref, got_ref, mixed_ref, series_ref, k_ref, v_ref, c_ref, own_ref, core_ref,
    gq_ref, gk_ref, gv_ref, gf_ref, q_buf, k_buf, v_buf, f_buf, sems, f_sem,
):
    chunks = sems.shape[1]
    width = q_buf.shape[1] // chunks
    slots = got_ref.shape[0]
    count = slots // chunks
    kind = table_ref[2, 0]
    copies = []

    def filter_taps():
        quarters = []
        for t in range(4):
            sources = [s ^ TURN_BACK for s in range(slots) if 2 * (s // 16) + s % 2 == t]
            quarters.append(sum(got_ref[s, 32:40, :].astype(F32) for s in sources))
        near = jnp.concatenate(swap_blocks(quarters), 0)
        pair = own_ref[512:576, :].astype(F32) + core_ref[512:576, :].astype(F32)
        f_buf[:, :SPAN] = ((near + pair[:32]) * scale).astype(BF16)
        f_buf[:, SPAN:] = (pair[32:] * scale).astype(BF16)
        copy = pltpu.make_async_copy(f_buf, gf_ref, f_sem.at[0])
        copy.start()
        copies.append(copy)

    for j in range(chunks):
        cols = slice(j * width, (j + 1) * width)
        place = (j ^ (TURN_BACK // count)) * count
        rows = got_ref[place:place + count, 0:32, :].reshape(width, SPAN)
        pair = jnp.transpose(rows).astype(F32)
        mixed = mixed_ref[:, cols] + jnp.where(kind == 2, pair, 0.0)
        series = series_ref[:, cols] + jnp.where(kind == 1, pair, 0.0)
        mixed = mixed.astype(BF16).astype(F32)
        series = series.astype(BF16).astype(F32)
        q_buf[:, cols] = (c_ref[:, cols].astype(F32) * mixed).astype(BF16)
        k_buf[:, cols] = (series * v_ref[:, cols].astype(F32)).astype(BF16)
        v_buf[:, cols] = (series * k_ref[:, cols].astype(F32)).astype(BF16)
        for i, (buf, ref) in enumerate(((q_buf, gq_ref), (k_buf, gk_ref), (v_buf, gv_ref))):
            copy = pltpu.make_async_copy(buf.at[:, cols], ref.at[:, cols], sems.at[i, j])
            copy.start()
            copies.append(copy)
        if j == 1:
            filter_taps()
    for copy in copies:
        copy.wait()


SMEM = pl.BlockSpec(memory_space=pltpu.SMEM)
VMEM = pl.BlockSpec(memory_space=pltpu.VMEM)
HBM = pl.BlockSpec(memory_space=pltpu.HBM)
ANY = pl.BlockSpec(memory_space=pl.ANY)
DMA = pltpu.SemaphoreType.DMA


def params(mebibytes=32):
    return pltpu.CompilerParams(vmem_limit_bytes=mebibytes * 1024 * 1024)


def cost(flops, moved):
    return pl.CostEstimate(flops=int(flops), bytes_accessed=int(moved), transcendentals=0)


def per_device(query, key, value, cotangent, filter_taps, span_slot, doc_lengths):
    parts = lax.axis_size("ctx")
    tokens, width = query.shape
    area = tokens * width
    pairs = parts - doc_lengths.shape[1]
    scale = float(tokens * parts * lax.axis_size("dp")) ** (-0.5)
    forward, inverse = transforms()

    def constant(matrix, axis):
        return jnp.asarray(np.concatenate(split_bf16(matrix), axis))

    fwd = constant(forward[:, :SPAN], 1)
    fwd_t = constant(forward[:, :SPAN].T, 0)
    inv = constant(inverse[:SPAN], 0)
    inv_t = constant(inverse[:SPAN].T, 1)
    tap_t = constant(np.roll(forward, -SPAN, 1).T, 0)
    lag_t = constant(np.roll(inverse, SPAN, 0).T, 1)
    core_swap = [(0, 1), (1, 0)]
    side_swap = [(c, c ^ 16) for c in range(parts)]
    cross_swap = [(c, c ^ 17) for c in range(parts)]
    next_swap = [(c, c ^ 1) for c in range(parts)]
    steps = width // 256
    taps_rows = filter_taps.T

    def exchange(array, turn):
        order = [[k ^ turn for k in range(parts)]]
        return lax.all_to_all(
            array, "ctx", split_axis=0, concat_axis=0, axis_index_groups=order, tiled=True
        )

    chunk = jax.ShapeDtypeStruct((parts, 40, SPAN), BF16)
    out = pl.pallas_call(
        send_kernel,
        out_shape=chunk,
        in_specs=[HBM] * 7,
        out_specs=HBM,
        scratch_shapes=[
            pltpu.SMEM(span_slot.shape, jnp.int32),
            pltpu.SMEM(doc_lengths.shape, jnp.int32),
            pltpu.VMEM(taps_rows.shape, BF16),
        ] + [pltpu.VMEM((tokens, width), BF16)] * 4 + [
            pltpu.VMEM(chunk.shape, BF16), DMA((3,)), DMA((4, 2)), DMA((2,)),
        ],
        compiler_params=params(60),
        cost_estimate=cost(2 * area, 8 * area),
        name="send",
    )(span_slot, doc_lengths, taps_rows, query, key, value, cotangent)
    got = exchange(out, TURN_OUT)

    give = pl.pallas_call(
        partial_kernel,
        out_shape=jax.ShapeDtypeStruct((4, parts * 8, SPAN), BF16),
        in_specs=[VMEM] * 6,
        out_specs=VMEM,
        compiler_params=params(),
        cost_estimate=cost(2e9, 10 * area),
        name="partial_taps",
    )(query, key, value, cotangent, fwd, inv)
    taken = lax.ppermute(give, "dp", core_swap)
    quarter = jax.ShapeDtypeStruct((parts * 8, SPAN), BF16)
    keep, side, near, cross = pl.pallas_call(
        share_kernel,
        out_shape=(jax.ShapeDtypeStruct(quarter.shape, F32), quarter, quarter, quarter),
        in_specs=[VMEM, VMEM],
        out_specs=(VMEM,) * 4,
        compiler_params=params(),
        cost_estimate=cost(area, 3 * area),
        name="share",
    )(give, taken)
    table, tap_spec = pl.pallas_call(
        tables_kernel,
        out_shape=(
            jax.ShapeDtypeStruct((3, 2 * pairs), jnp.int32),
            jax.ShapeDtypeStruct((32, PTS), F32),
        ),
        in_specs=[SMEM, SMEM, VMEM, VMEM, ANY],
        out_specs=(SMEM, VMEM),
        scratch_shapes=[pltpu.SMEM((parts,), jnp.int32)],
        compiler_params=params(),
        cost_estimate=cost(area, area),
        name="tables",
    )(span_slot, doc_lengths, taps_rows, tap_t, give)
    side = lax.ppermute(side, "ctx", side_swap)
    near = lax.ppermute(near, "ctx", next_swap)
    cross = lax.ppermute(cross, "ctx", cross_swap)

    back = pl.pallas_call(
        pair_kernel,
        out_shape=jax.ShapeDtypeStruct((parts, 32, SPAN), BF16),
        in_specs=[SMEM] + [VMEM] * 4,
        out_specs=VMEM,
        compiler_params=params(),
        cost_estimate=cost(1e9, 8 * area),
        name="pair",
    )(table, got, tap_spec, fwd_t, inv_t)
    back = pl.pallas_call(
        load_kernel,
        out_shape=chunk,
        in_specs=[VMEM] * 5,
        out_specs=HBM,
        scratch_shapes=[pltpu.VMEM(chunk.shape, BF16), DMA((2,))],
        compiler_params=params(),
        cost_estimate=cost(area, 4 * area),
        name="load",
    )(back, keep, cross, near, side)
    landed = exchange(back, TURN_BACK)

    own = got[:, 32:40, :].reshape(parts * 8, SPAN)
    pair_taps, xs, gs = pl.pallas_call(
        pair_taps_kernel,
        out_shape=(jax.ShapeDtypeStruct((64, SPAN), BF16),)
        + (jax.ShapeDtypeStruct((PTS, width), F32),) * 2,
        in_specs=[SMEM] + [VMEM] * 8,
        out_specs=(VMEM,) * 3,
        compiler_params=params(),
        cost_estimate=cost(1e9, 6 * area),
        name="pair_taps",
    )(table, got, query, key, value, cotangent, fwd_t, fwd, lag_t)
    own = jnp.concatenate([own, lax.ppermute(own, "ctx", side_swap), pair_taps], 0)
    core = lax.ppermute(own, "dp", core_swap)
    mixed, series = pl.pallas_call(
        local_kernel,
        out_shape=(jax.ShapeDtypeStruct((tokens, width), F32),) * 2,
        in_specs=[VMEM] * 6,
        out_specs=(VMEM, VMEM),
        compiler_params=params(),
        cost_estimate=cost(3e9, 20 * area),
        name="local",
    )(own, core, xs, gs, fwd, inv)

    result = jax.ShapeDtypeStruct((tokens, width), BF16)
    *grads, grad_filter = pl.pallas_call(
        functools.partial(finish_kernel, scale),
        out_shape=(result,) * 3 + (jax.ShapeDtypeStruct((32, PTS), BF16),),
        in_specs=[SMEM] + [VMEM] * 8,
        out_specs=(HBM,) * 4,
        scratch_shapes=[pltpu.VMEM((tokens, width), BF16)] * 3
        + [pltpu.VMEM((32, PTS), BF16), DMA((3, steps)), DMA((1,))],
        compiler_params=params(),
        cost_estimate=cost(10 * area, 20 * area),
        name="finish",
    )(table, landed, mixed, series, key, value, cotangent, own, core)
    return (*grads, grad_filter.T)


def solution(mesh):
    return jax.shard_map(
        per_device,
        mesh=mesh,
        in_specs=(
            P(("dp", "ctx"), "ch"),
            P(("dp", "ctx"), "ch"),
            P(("dp", "ctx"), "ch"),
            P(("dp", "ctx"), "ch"),
            P(None, ("ch", "ctx")),
            P("dp", None),
            P("dp", None),
        ),
        out_specs=(
            P(("dp", "ctx"), "ch"),
            P(("dp", "ctx"), "ch"),
            P(("dp", "ctx"), "ch"),
            P(None, ("ch", "ctx")),
        ),
        check_vma=False,
    )
```
